128 devices in a mesh: grp: 16 (over y, x_lo, core), head: 8 (over x_hi, z).
Axes of the slice: x: 4 (x_hi: 2, x_lo: 2; x = x_hi * 2 + x_lo), y: 4, z: 4, core: 2. Of those that a mesh axis runs over, the one named last changes fastest.
Arguments:
- queries: bfloat16 [16, 128, 40, 128], P('grp', None, 'head'), may hold values from -8 to 8
- response_keys: bfloat16 [16, 128, 8, 128], P('grp', None, 'head'), may hold values from -6 to 6
- response_values: bfloat16 [16, 128, 8, 128], P('grp', None, 'head'), may hold values from -6 to 6
- prompt_keys: bfloat16 [32768, 8, 128], P('grp', 'head'), may hold values from -8 to 8
- prompt_value_rows: bfloat16 [32768, 8, 128], P('grp', 'head'), may hold values from -6 to 6
- w_out: bfloat16 [5120, 5120], P('head'), may hold values from -0.15625 to 0.15625
- prompt_len: int32 [1], replicated, may hold values from 16384 to 32768
- resp_len: int32 [16], P('grp'), may hold values from 32 to 128, as said below
Outputs:
- output: bfloat16 [16, 128, 5120], P('grp', 'head')
The draws below stay inside these ranges and needn't reach their ends.
Inputs may be any that keep to these rules, and one draw needn't show every extreme that they name: `resp_len`: one response in every draw has all 128 tokens.
All inputs are finite; a program needn't handle non-finite values.
Results may differ from the reference program's by a relative error of at most 0.019.
Values may be sent and summed in bfloat16 or wider, within the bound.
No kernel may reach another device: no remote copies, remote signals or barrier semaphores. Data moves between devices by JAX's collectives and lax.ppermute only.
A program may use at most 64 MiB of HBM per device.

```python
import math
import jax
import jax.numpy as jnp
from jax import lax

D = 5120
QUERY_HEADS = 40
KEY_VALUE_HEADS = 8
HEAD_DIMENSION = 128
RESPONSE_LENGTH = 128
PROMPT_LENGTH = 32768
RESPONSE_COUNT = 16
N_HEAD = 8


def draw_queries(key, part):
    key = jax.random.fold_in(key, 1)
    array_shape = (RESPONSE_COUNT, RESPONSE_LENGTH, QUERY_HEADS, HEAD_DIMENSION)
    values = 1.5 * jax.random.truncated_normal(key, -4.0, 4.0, array_shape, jnp.float32)
    return values.astype(jnp.bfloat16)


def draw_prompt_keys(key, part):
    key = jax.random.fold_in(key, 2)
    array_shape = (PROMPT_LENGTH, KEY_VALUE_HEADS, HEAD_DIMENSION)
    values = 1.5 * jax.random.truncated_normal(key, -4.0, 4.0, array_shape, jnp.float32)
    return values.astype(jnp.bfloat16)


def draw_resp_len(key, part):
    key = jax.random.fold_in(key, 3)
    length_key, full_key = jax.random.split(key)
    lengths = jax.random.randint(length_key, (RESPONSE_COUNT,), RESPONSE_LENGTH // 4, RESPONSE_LENGTH + 1)
    full_one = jax.random.randint(full_key, (), 0, RESPONSE_COUNT)
    return jnp.where(jnp.arange(RESPONSE_COUNT) == full_one, RESPONSE_LENGTH, lengths).astype(jnp.int32)


def block_scale(own_key, extent, pieces, least, high):
    def one(position, blocks):
        steps = jax.random.uniform(jax.random.fold_in(jax.random.fold_in(own_key, 6), position), (blocks,), jnp.float32, least / len(pieces), high / len(pieces))
        return jnp.repeat(jnp.exp(steps), extent[position] // blocks).reshape((-1,) + (1,) * (len(extent) - position - 1))

    gain = one(*pieces[0])
    for cut in pieces[1:]:
        gain = gain * one(*cut)
    return gain


def bell_draw(stream_key, extent, spread, bound, shards=(), held_as=jnp.bfloat16):
    result = jax.random.normal(stream_key, extent, jnp.float32) * spread
    if len(shards) > 0:
        result = block_scale(stream_key, extent, shards, -0.22, 0.18) * result
    return jnp.clip(result, min=-bound, max=bound).astype(held_as)


def setup_inputs(seed: int = 0) -> dict:
    keys = jax.random.split(jax.random.key(seed), 9)
    return {
        "queries": draw_queries(jax.random.fold_in(keys[8], 71), 0),
        "response_keys": bell_draw(keys[1], (RESPONSE_COUNT, RESPONSE_LENGTH, KEY_VALUE_HEADS, HEAD_DIMENSION), 1.5, 6.0, ((0, 16), (2, 8))),
        "response_values": bell_draw(keys[2], (RESPONSE_COUNT, RESPONSE_LENGTH, KEY_VALUE_HEADS, HEAD_DIMENSION), 1.0, 6.0, ((0, 16), (2, 8))),
        "prompt_keys": draw_prompt_keys(jax.random.fold_in(keys[8], 71), 0),
        "prompt_value_rows": bell_draw(keys[4], (PROMPT_LENGTH, KEY_VALUE_HEADS, HEAD_DIMENSION), 1.0, 6.0, ((0, 16), (1, 8))),
        "w_out": bell_draw(keys[5], (QUERY_HEADS * HEAD_DIMENSION, D), (QUERY_HEADS * HEAD_DIMENSION // 4) ** -0.5, 0.15625, ((0, 8),)),
        "prompt_len": jax.random.randint(keys[6], (1,), PROMPT_LENGTH // 2, PROMPT_LENGTH + 1).astype(jnp.int32),
        "resp_len": draw_resp_len(jax.random.fold_in(keys[8], 71), 0),
    }


def reference(queries, response_keys, response_values, prompt_keys, prompt_value_rows, w_out, prompt_len, resp_len):
    heads_per_group = QUERY_HEADS // KEY_VALUE_HEADS
    scaling = 1.0 / math.sqrt(HEAD_DIMENSION)
    highest = lax.Precision.HIGHEST
    key_pos = jnp.arange(PROMPT_LENGTH, dtype=jnp.int32)
    prompt_ok = key_pos < prompt_len[0]
    step_pos = jnp.arange(RESPONSE_LENGTH, dtype=jnp.int32)
    causal = step_pos[None, :] <= step_pos[:, None]

    def one_response(inputs):
        query_one, key_one, value_one = inputs

        def single_group(group_id):
            query_set = lax.dynamic_slice_in_dim(query_one, (group_id * heads_per_group).astype(jnp.int32), heads_per_group, 1).astype(jnp.float32)
            key_prompt = lax.dynamic_index_in_dim(prompt_keys, group_id, 1, keepdims=False).astype(jnp.float32)
            value_prompt = lax.dynamic_index_in_dim(prompt_value_rows, group_id, 1, keepdims=False).astype(jnp.float32)
            key_own = lax.dynamic_index_in_dim(key_one, group_id, 1, keepdims=False).astype(jnp.float32)
            value_own = lax.dynamic_index_in_dim(value_one, group_id, 1, keepdims=False).astype(jnp.float32)
            score_prompt = jnp.einsum('tid,jd->tij', query_set, key_prompt, precision=highest) * scaling
            score_prompt = jnp.where(prompt_ok[None, None, :], score_prompt, -jnp.inf)
            score_own = jnp.einsum('tid,sd->tis', query_set, key_own, precision=highest) * scaling
            score_own = jnp.where(causal[:, None, :], score_own, -jnp.inf)
            peak = jnp.maximum(lax.optimization_barrier(jnp.max(score_prompt, axis=-1)), lax.optimization_barrier(jnp.max(score_own, axis=-1)))
            weight_prompt = jnp.exp(score_prompt - peak[..., None])
            weight_own = jnp.exp(score_own - peak[..., None])
            weight_sum = lax.optimization_barrier(jnp.sum(weight_prompt, axis=-1)) + lax.optimization_barrier(jnp.sum(weight_own, axis=-1))
            rounded_prompt = lax.optimization_barrier(weight_prompt.astype(jnp.bfloat16)).astype(jnp.float32)
            rounded_own = lax.optimization_barrier(weight_own.astype(jnp.bfloat16)).astype(jnp.float32)
            mixed = jnp.einsum('tij,jd->tid', rounded_prompt, value_prompt, precision=highest)
            mixed = mixed + jnp.einsum('tis,sd->tid', rounded_own, value_own, precision=highest)
            return mixed / weight_sum[..., None]
        grouped_rows = lax.map(single_group, jnp.arange(KEY_VALUE_HEADS, dtype=jnp.int32))
        return jnp.transpose(grouped_rows, (1, 0, 2, 3)).reshape(RESPONSE_LENGTH, QUERY_HEADS * HEAD_DIMENSION).astype(jnp.bfloat16)
    attended = lax.map(one_response, (queries, response_keys, response_values))
    columns = QUERY_HEADS // N_HEAD * HEAD_DIMENSION

    def add_part(column_set, summed):
        first_col = (column_set * columns).astype(jnp.int32)
        block_cols = lax.dynamic_slice_in_dim(attended, first_col, columns, 2).astype(jnp.float32)
        rows_w = lax.dynamic_slice_in_dim(w_out, first_col, columns, 0).astype(jnp.float32)
        partial_sum = jnp.einsum('nrc,cd->nrd', block_cols, rows_w, precision=highest)
        rounded = lax.optimization_barrier(partial_sum.astype(jnp.bfloat16))
        return summed + rounded.astype(jnp.float32)
    projected = lax.fori_loop(0, N_HEAD, add_part, jnp.zeros((RESPONSE_COUNT, RESPONSE_LENGTH, D), jnp.float32))
    live_rows = step_pos[None, :] < resp_len[:, None]
    return jnp.where(live_rows[..., None], projected, 0.0).astype(jnp.bfloat16)
```

```python
import math

import jax
import jax.numpy as jnp
from jax import lax
from jax.experimental import pallas as pl
from jax.experimental.pallas import tpu as pltpu
from jax.sharding import PartitionSpec as P

F32, BF16 = jnp.float32, jnp.bfloat16
LANES = 128
BLOCK_ROWS = 512
TAIL = 16
TO_BASE_2 = math.log2(math.e)
UNSEEN = -1e30
NT = (((1,), (1,)), ((), ()))


def scaled_halves(q, scale):
    scaled = q.astype(F32) * scale
    high = scaled.astype(BF16)
    low = (scaled - high.astype(F32)).astype(BF16)
    return jnp.concatenate([high, low], axis=1)


def diagonal_row(tile):
    eye = lax.broadcasted_iota(jnp.int32, tile.shape, 0) == lax.broadcasted_iota(
        jnp.int32, tile.shape, 1
    )
    return jnp.sum(jnp.where(eye, tile, 0.0), axis=0, keepdims=True)


def prompt_kernel(
    valid_ref, q_ref, k0_ref, k1_ref, v0_ref, v1_ref, out_ref, packed, mixed, logs, acc
):
    responses, rows, width = q_ref.shape
    rows = rows - TAIL
    heads = rows // LANES
    scale = TO_BASE_2 / math.sqrt(width)
    keys = k0_ref.shape[0]
    ones = jnp.ones((LANES, LANES), BF16)

    offset = jnp.int32(0)
    offsets = []
    for i in range(responses):
        offsets.append(offset)
        packed[pl.ds(pl.multiple_of(offset, 16), rows), :] = q_ref[i, :rows, :]
        length = jnp.max(q_ref[i, rows:, :].astype(F32)).astype(jnp.int32)
        offset = offset + (length * heads + 15) // 16 * 16
    total = offset

    key_norm = jnp.zeros((1, LANES), F32)
    for k_ref in (k0_ref, k1_ref):
        k = k_ref[...]
        squares = jnp.dot(k * k, ones, preferred_element_type=F32)
        key_norm = jnp.maximum(key_norm, jnp.max(squares, axis=0, keepdims=True))
    key_norm = jnp.sqrt(key_norm) * (scale * 1.01)
    some_valid = jnp.maximum(valid_ref[0], valid_ref[1]) > 0

    def block(b, carry):
        here = pl.ds(pl.multiple_of(b * BLOCK_ROWS, BLOCK_ROWS), BLOCK_ROWS)
        q = packed[here, :]
        halves = scaled_halves(q, scale)
        bound = (
            jnp.sqrt(jnp.dot(q * q, ones, preferred_element_type=F32)) * key_norm
        )

        def scores(k):
            return lax.dot_general(
                halves, jnp.concatenate([k, k], axis=1), NT, preferred_element_type=F32
            )

        def run(peak):
            acc[...] = jnp.zeros_like(acc)
            spread = jnp.concatenate([peak] * (keys // LANES), axis=1)
            for part, (k_ref, v_ref) in enumerate(((k0_ref, v0_ref), (k1_ref, v1_ref))):
                valid = valid_ref[part]

                def piece(masked):
                    weights = jnp.exp2(scores(k_ref[...]) - spread)
                    if masked:
                        position = lax.broadcasted_iota(jnp.int32, weights.shape, 1)
                        weights = jnp.where(position < valid, weights, 0.0)
                    v = jnp.concatenate([v_ref[...], jnp.ones((keys, LANES), BF16)], axis=1)
                    acc[...] += jnp.dot(
                        weights.astype(BF16), v, preferred_element_type=F32
                    )

                @pl.when(valid >= keys)
                def _():
                    piece(False)

                @pl.when(jnp.logical_and(valid < keys, valid > 0))
                def _():
                    piece(True)

            weight_sum = acc[:, LANES:]
            mixed[here, :] = acc[:, :LANES] / weight_sum
            logs[here, :] = jnp.log2(weight_sum) + peak

        run(bound)
        lowest = jnp.min(acc[:, LANES:])

        @pl.when(jnp.logical_and(some_valid, jnp.logical_not(lowest > 2.0**-90)))
        def _():
            def highest(part, k_ref, peak):
                valid = valid_ref[part]
                step = 256

                def fold(c, peak):
                    start = pl.multiple_of(c * step, step)
                    s = scores(k_ref[pl.ds(start, step), :])
                    position = start + lax.broadcasted_iota(jnp.int32, s.shape, 1)
                    s = jnp.where(position < valid, s, UNSEEN)
                    return jnp.maximum(peak, jnp.max(s, axis=1, keepdims=True))

                return lax.fori_loop(0, (valid + step - 1) // step, fold, peak)

            peak = jnp.full((BLOCK_ROWS, 1), UNSEEN, F32)
            peak = highest(0, k0_ref, peak)
            peak = highest(1, k1_ref, peak)
            run(jnp.broadcast_to(peak, (BLOCK_ROWS, LANES)))

        @pl.when(jnp.logical_not(some_valid))
        def _():
            mixed[here, :] = jnp.zeros((BLOCK_ROWS, width), F32)
            logs[here, :] = jnp.full((BLOCK_ROWS, LANES), UNSEEN, F32)

        return carry

    lax.fori_loop(0, (total + BLOCK_ROWS - 1) // BLOCK_ROWS, block, 0)

    for i in range(responses):
        start = pl.multiple_of(offsets[i], 16)
        out_ref[i, :rows, :] = mixed[pl.ds(start, rows), :].astype(BF16)
        lines = []
        for j in range(heads):
            lines.append(
                diagonal_row(logs[pl.ds(pl.multiple_of(start + j * LANES, 16), LANES), :])
            )
        log = jnp.concatenate(lines, axis=0)
        high = log.astype(BF16).astype(F32)
        middle = (log - high).astype(BF16).astype(F32)
        low = log - high - middle
        spare = jnp.zeros((TAIL - 3 * heads, LANES), F32)
        out_ref[i, rows:, :] = jnp.concatenate([high, middle, low, spare], axis=0).astype(BF16)


def prompt_part(valid, q_all, k0, k1, v0, v1):
    responses, rows, width = q_all.shape
    vmem = pl.BlockSpec(memory_space=pltpu.VMEM)
    smem = pl.BlockSpec(memory_space=pltpu.SMEM)
    packed_rows = responses * (rows - TAIL) + max(BLOCK_ROWS, rows)
    return pl.pallas_call(
        prompt_kernel,
        out_shape=jax.ShapeDtypeStruct(q_all.shape, BF16),
        in_specs=[smem] + [vmem] * 5,
        out_specs=vmem,
        scratch_shapes=[
            pltpu.VMEM((packed_rows, width), BF16),
            pltpu.VMEM((packed_rows, width), F32),
            pltpu.VMEM((packed_rows, LANES), F32),
            pltpu.VMEM((BLOCK_ROWS, width + LANES), F32),
        ],
        compiler_params=pltpu.CompilerParams(vmem_limit_bytes=56 * 2**20),
        cost_estimate=pl.CostEstimate(
            flops=14 * 10**9, bytes_accessed=5 * 10**6, transcendentals=14 * 10**6
        ),
        name="prompt_part",
    )(valid, q_all, k0, k1, v0, v1)


def own_kernel(q_ref, k_ref, v_ref, mixed_ref, log_ref):
    rows, width = q_ref.shape
    heads = rows // LANES
    halves = scaled_halves(q_ref[...], TO_BASE_2 / math.sqrt(width))
    k = k_ref[...]
    s = lax.dot_general(
        halves, jnp.concatenate([k, k], axis=1), NT, preferred_element_type=F32
    )
    row = lax.broadcasted_iota(jnp.int32, s.shape, 0)
    position = lax.broadcasted_iota(jnp.int32, s.shape, 1)
    s = jnp.where(position * heads <= row, s, UNSEEN)
    peak = jnp.max(s, axis=1, keepdims=True)
    weights = jnp.exp2(s - peak)
    weight_sum = jnp.sum(weights, axis=1, keepdims=True)
    mixed_ref[...] = (
        jnp.dot(weights.astype(BF16), v_ref[...], preferred_element_type=F32) / weight_sum
    )
    log = jnp.broadcast_to(jnp.log2(weight_sum) + peak, (rows, LANES))
    for j in range(heads):
        log_ref[j : j + 1, :] = diagonal_row(log[j * LANES : (j + 1) * LANES, :])


def own_part(q, k, v):
    vmem = pl.BlockSpec(memory_space=pltpu.VMEM)
    return pl.pallas_call(
        own_kernel,
        out_shape=(
            jax.ShapeDtypeStruct(q.shape, F32),
            jax.ShapeDtypeStruct((8, LANES), F32),
        ),
        in_specs=[vmem] * 3,
        out_specs=(vmem, vmem),
        cost_estimate=pl.CostEstimate(
            flops=10**8, bytes_accessed=10**6, transcendentals=10**5
        ),
        name="own_part",
    )(q, k, v)


def project_kernel(parts_ref, mixed_ref, log_ref, w_hbm, out_ref, w_ref, attended, sems):
    count, rows, width = parts_ref.shape
    rows = rows - TAIL
    heads = rows // LANES
    chunks, _, columns = w_ref.shape
    copies = [
        pltpu.make_async_copy(
            w_hbm.at[:, pl.ds(c * columns, columns)], w_ref.at[c], sems.at[c]
        )
        for c in range(chunks)
    ]
    for copy in copies:
        copy.start()
    logs = [log_ref[:heads, :]]
    for p in range(count):
        tail = parts_ref[p, rows:, :].astype(F32)
        logs.append(
            tail[:heads] + tail[heads : 2 * heads] + tail[2 * heads : 3 * heads]
        )
    peak = logs[0]
    for log in logs[1:]:
        peak = jnp.maximum(peak, log)
    shares = [jnp.exp2(log - peak) for log in logs]
    total = shares[0]
    for share in shares[1:]:
        total = total + share
    shares = [share / total for share in shares]
    for j in range(heads):
        lines = [share[j : j + 1, :] for share in shares]
        lines.append(jnp.zeros((LANES - len(lines), LANES), F32))
        by_row = jnp.concatenate(lines, axis=0).T
        here = slice(j * LANES, (j + 1) * LANES)
        value = mixed_ref[here, :] * by_row[:, 0:1]
        for p in range(count):
            value = value + parts_ref[p, here, :].astype(F32) * by_row[:, p + 1 : p + 2]
        attended[here, :] = value
    tokens = rows // heads
    wide = jnp.concatenate(
        [attended[pl.ds(h, tokens, stride=heads), :].astype(BF16) for h in range(heads)],
        axis=1,
    )
    for c in range(chunks):
        copies[c].wait()
        out_ref[:, c * columns : (c + 1) * columns] = jnp.dot(
            wide, w_ref[c], preferred_element_type=F32
        ).astype(BF16)


def project(parts, mixed, log, w_out):
    rows = mixed.shape[0]
    depth, columns = w_out.shape
    heads = depth // mixed.shape[1]
    chunks = 4
    vmem = pl.BlockSpec(memory_space=pltpu.VMEM)
    return pl.pallas_call(
        project_kernel,
        out_shape=jax.ShapeDtypeStruct((rows // heads, columns), BF16),
        in_specs=[vmem, vmem, vmem, pl.BlockSpec(memory_space=pl.ANY)],
        out_specs=vmem,
        scratch_shapes=[
            pltpu.VMEM((chunks, depth, columns // chunks), BF16),
            pltpu.VMEM(mixed.shape, F32),
            pltpu.SemaphoreType.DMA((chunks,)),
        ],
        compiler_params=pltpu.CompilerParams(vmem_limit_bytes=48 * 2**20),
        cost_estimate=pl.CostEstimate(
            flops=10**9, bytes_accessed=10**7, transcendentals=10**5
        ),
        name="project",
    )(parts, mixed, log, w_out)


def per_device(
    queries,
    response_keys,
    response_values,
    prompt_keys,
    prompt_value_rows,
    w_out,
    prompt_len,
    resp_len,
):
    tokens, heads, width = queries.shape[1:]
    rows = tokens * heads
    devices = lax.axis_size("grp")
    pairs = devices // 2
    same_core = [[2 * i + c for i in range(pairs)] for c in range(2)]
    swap = [(i, i ^ 1) for i in range(devices)]
    me = lax.axis_index("grp")

    q = queries[0].reshape(rows, width)
    k_mine = prompt_keys.reshape(-1, width)
    v_mine = prompt_value_rows.reshape(-1, width)
    keys = k_mine.shape[0]
    k_other = lax.ppermute(k_mine, "grp", swap)
    v_other = lax.ppermute(v_mine, "grp", swap)
    tail = jnp.broadcast_to(resp_len.astype(BF16)[:, None], (TAIL, width))
    sent = jnp.broadcast_to(jnp.concatenate([q, tail], axis=0)[None], (pairs, rows + TAIL, width))
    q_all = lax.all_to_all(
        sent, "grp", 0, 0, tiled=True, axis_index_groups=same_core
    )
    mixed, log = own_part(
        q, response_keys.reshape(tokens, width), response_values.reshape(tokens, width)
    )
    starts = jnp.stack([me, me ^ 1]).astype(jnp.int32) * keys
    valid = jnp.clip(prompt_len[0] - starts, 0, keys)
    parts = prompt_part(valid, q_all, k_mine, k_other, v_mine, v_other)
    parts = lax.all_to_all(parts, "grp", 0, 0, tiled=True, axis_index_groups=same_core)
    partial = project(parts, mixed, log, w_out)

    splits = lax.axis_size("head")
    rows_out = tokens // splits
    pieces = lax.all_to_all(
        partial.reshape(splits, rows_out, -1), "head", 0, 0, tiled=True
    )
    summed = jnp.sum(pieces.astype(F32), axis=0)
    first_out = lax.axis_index("head") * rows_out
    live_rows = first_out + jnp.arange(rows_out, dtype=jnp.int32) < resp_len[0]
    return jnp.where(live_rows[:, None], summed, 0.0).astype(BF16)[None]


def solution(mesh):
    in_specs = (
        P("grp", None, "head", None),
        P("grp", None, "head", None),
        P("grp", None, "head", None),
        P("grp", "head", None),
        P("grp", "head", None),
        P("head", None),
        P(),
        P("grp"),
    )
    return jax.shard_map(
        per_device,
        mesh=mesh,
        in_specs=in_specs,
        out_specs=P("grp", "head", None),
        check_vma=False,
    )
```

```python
import functools
import math

import jax
import jax.numpy as jnp
from jax import lax
from jax.experimental import pallas as pl
from jax.experimental.pallas import tpu as pltpu
from jax.sharding import PartitionSpec as P

F32, BF16 = jnp.float32, jnp.bfloat16
LANES = 128
BLOCK_ROWS = 512
TAIL = 16
PROMPT_VMEM = 28 * 2**20
SMALL_VMEM = 16 * 2**20
PROJECT_VMEM = 48 * 2**20
NEAR = 4
TO_BASE_2 = math.log2(math.e)
UNSEEN = -1e30
NT = (((1,), (1,)), ((), ()))


def scaled_halves(q, scale):
    scaled = q.astype(F32) * scale
    high = scaled.astype(BF16)
    low = (scaled - high.astype(F32)).astype(BF16)
    return jnp.concatenate([high, low], axis=1)


def diagonal_row(tile):
    eye = lax.broadcasted_iota(jnp.int32, tile.shape, 0) == lax.broadcasted_iota(
        jnp.int32, tile.shape, 1
    )
    return jnp.sum(jnp.where(eye, tile, 0.0), axis=0, keepdims=True)


def log_lines(logs, start, count):
    lines = []
    for j in range(count):
        tile = logs[pl.ds(pl.multiple_of(start + j * LANES, 16), LANES), :]
        lines.append(diagonal_row(tile))
    log = jnp.concatenate(lines, axis=0)
    high = log.astype(BF16).astype(F32)
    middle = (log - high).astype(BF16).astype(F32)
    low = log - high - middle
    spare = jnp.zeros((TAIL - 3 * count, LANES), F32)
    return jnp.concatenate([high, middle, low, spare], axis=0).astype(BF16)


def prompt_kernel(responses, continued, valid_ref, place_ref, *refs):
    q_refs, refs = refs[:responses], refs[responses:]
    norm_ref, k_ref, v_ref = refs[:3]
    if continued:
        mixed_kept, logs_kept, out_ref, packed, mixed, logs, acc, sems = refs[3:]
    else:
        mixed_kept, logs_kept, done_ref, packed, mixed, logs, acc, sems = refs[3:]
    keys, width = k_ref.shape
    keys = keys // 2
    rows = q_refs[0].shape[0] - TAIL
    heads = rows // LANES
    scale = TO_BASE_2 / math.sqrt(width)
    ones = jnp.ones((LANES, LANES), BF16)
    key_norm = norm_ref[0:1, :]

    lengths = [
        jnp.max(q_ref[rows:, :].astype(F32)).astype(jnp.int32) for q_ref in q_refs
    ]
    offset = jnp.int32(0)
    offsets = []
    for i, q_ref in enumerate(q_refs):
        offsets.append(offset)
        packed[pl.ds(pl.multiple_of(offset, 16), rows), :] = q_ref[:rows, :]
        offset = offset + (lengths[i] * heads + 15) // 16 * 16
    total = offset
    packed[pl.ds(pl.multiple_of(offsets[-1], 16) + rows, BLOCK_ROWS), :] = jnp.zeros(
        (BLOCK_ROWS, width), BF16
    )
    valid = (valid_ref[0], valid_ref[1])
    both_valid = jnp.minimum(*valid) > 0
    some_valid = jnp.maximum(*valid) > 0
    def state_copies(b, count):
        here = pl.ds(pl.multiple_of(b * BLOCK_ROWS, BLOCK_ROWS), count)
        pairs = ((mixed, mixed_kept), (logs, logs_kept))
        return [
            pltpu.make_async_copy(kept.at[here, :], ref.at[here, :], sems.at[i, b])
            if continued
            else pltpu.make_async_copy(ref.at[here, :], kept.at[here, :], sems.at[i, b])
            for i, (ref, kept) in enumerate(pairs)
        ]

    def block(b, count):
        here = pl.ds(pl.multiple_of(b * BLOCK_ROWS, BLOCK_ROWS), count)
        if continued:
            for copy in state_copies(b, count):
                copy.wait()

        def query():
            q = packed[here, :]
            squares = jnp.dot(q * q, ones, preferred_element_type=F32)
            return scaled_halves(q, scale), jnp.sqrt(squares) * key_norm

        def scores(halves, k):
            return lax.dot_general(
                halves, jnp.concatenate([k, k], axis=1), NT, preferred_element_type=F32
            )

        def finish(total, peak):
            weight_sum = total[:, LANES:]
            value = total[:, :LANES] / weight_sum
            log = jnp.log2(weight_sum) + peak
            if continued:
                value, log = join(mixed[here, :], logs[here, :], value, log)
            mixed[here, :] = value
            logs[here, :] = log

        def exact():
            halves, _ = query()
            step = 256

            def over_keys(body, carry):
                for part in range(2):

                    def one(c, carry):
                        start = pl.multiple_of(c * step, step)
                        these = pl.ds(part * keys + start, step)
                        s = scores(halves, k_ref[these, :])
                        position = start + lax.broadcasted_iota(jnp.int32, s.shape, 1)
                        s = jnp.where(position < valid[part], s, UNSEEN)
                        return body(s, v_ref[these, :], carry)

                    carry = lax.fori_loop(0, (valid[part] + step - 1) // step, one, carry)
                return carry

            def fold(s, v, peak):
                return jnp.maximum(peak, jnp.max(s, axis=1, keepdims=True))

            peak = over_keys(fold, jnp.full((count, 1), UNSEEN, F32))
            acc[:count, :] = jnp.zeros((count, width + LANES), F32)

            def add(s, v, carry):
                weights = jnp.exp2(s - peak).astype(BF16)
                acc[:count, :] += jnp.dot(weights, v, preferred_element_type=F32)
                return carry

            over_keys(add, 0)
            finish(acc[:count, :], jnp.broadcast_to(peak, (count, LANES)))

        def quick(start, size):
            halves, bound = query()
            these = pl.ds(start, size)
            spread = jnp.concatenate([bound] * (size // LANES), axis=1)
            weights = jnp.exp2(scores(halves, k_ref[these, :]) - spread).astype(BF16)
            total = jnp.dot(weights, v_ref[these, :], preferred_element_type=F32)
            fine = jnp.min(total[:, LANES:]) > 2.0**-90
            if not continued:
                finish(total, bound)
            else:
                acc[:count, :] = total

                @pl.when(fine)
                def _():
                    finish(acc[:count, :], bound)

            @pl.when(jnp.logical_not(fine))
            def _():
                exact()

        @pl.when(both_valid)
        def _():
            quick(0, 2 * keys)

        @pl.when(jnp.logical_and(some_valid, jnp.logical_not(both_valid)))
        def _():
            quick(pl.multiple_of(jnp.where(valid[0] > 0, 0, keys), keys), keys)

        @pl.when(jnp.logical_not(some_valid))
        def _():
            if not continued:
                mixed[here, :] = jnp.zeros((count, width), F32)
                logs[here, :] = jnp.full((count, LANES), UNSEEN, F32)

    half = BLOCK_ROWS // 2
    spare_rows = total % BLOCK_ROWS
    big = total // BLOCK_ROWS + (spare_rows > half).astype(jnp.int32)

    last = total > big * BLOCK_ROWS

    def each(do):
        @pl.loop(0, big)
        def _(b):
            do(b, BLOCK_ROWS)

        @pl.when(last)
        def _():
            do(big, half)

    def start(b, count):
        for copy in state_copies(b, count):
            copy.start()

    def finish_copies(b, count):
        for copy in state_copies(b, count):
            copy.wait()

    if continued:
        each(start)
        each(block)
    else:

        def block_and_start(b, count):
            block(b, count)
            start(b, count)

        each(block_and_start)
        each(finish_copies)

    if not continued:
        done_ref[...] = jnp.zeros_like(done_ref)
    else:
        for i in range(responses):
            start = pl.multiple_of(offsets[i], 16)
            place = (place_ref[0] + i) % responses
            out_ref[place, :rows, :] = mixed[pl.ds(start, rows), :].astype(BF16)
            out_ref[place, rows:, :] = log_lines(logs, start, pl.cdiv(rows, LANES))


def join(value0, log0, value1, log1):
    peak = jnp.maximum(log0, log1)
    weight0, weight1 = jnp.exp2(log0 - peak), jnp.exp2(log1 - peak)
    total = weight0 + weight1
    return (value0 * weight0 + value1 * weight1) / total, peak + jnp.log2(total)


def prompt_part(valid, place, queries, norm, k, v, before=None):
    responses = len(queries)
    rows, width = queries[0].shape
    vmem = pl.BlockSpec(memory_space=pltpu.VMEM)
    smem = pl.BlockSpec(memory_space=pltpu.SMEM)
    packed_rows = responses * (rows - TAIL) + BLOCK_ROWS + LANES
    state = [(packed_rows, width), (packed_rows, LANES)]
    operands = [valid, place, *queries, norm, k, v]
    scratch = [pltpu.VMEM((packed_rows, width), BF16)]
    scratch += [pltpu.VMEM(shape, F32) for shape in state]
    whole = pl.BlockSpec(memory_space=pl.ANY)
    in_specs = [smem] * 2 + [vmem] * (responses + 3)
    if before is None:
        out_shape = tuple(jax.ShapeDtypeStruct(shape, F32) for shape in state + [(8, LANES)])
        out_specs = (whole, whole, vmem)
    else:
        operands += list(before)
        in_specs += [whole] * 2
        out_shape = jax.ShapeDtypeStruct((responses, rows, width), BF16)
        out_specs = vmem
    return pl.pallas_call(
        functools.partial(prompt_kernel, responses, before is not None),
        out_shape=out_shape,
        in_specs=in_specs,
        out_specs=out_specs,
        scratch_shapes=scratch
        + [
            pltpu.VMEM((BLOCK_ROWS, width + LANES), F32),
            pltpu.SemaphoreType.DMA((2, pl.cdiv(packed_rows, BLOCK_ROWS))),
        ],
        compiler_params=pltpu.CompilerParams(vmem_limit_bytes=PROMPT_VMEM),
        cost_estimate=pl.CostEstimate(
            flops=10**8, bytes_accessed=10**6, transcendentals=10**5
        ),
        name="prompt_part",
    )(*operands)


def key_kernel(valid_ref, k0_ref, k1_ref, v0_ref, v1_ref, norm_ref, k_ref, v_ref):
    keys, width = k0_ref.shape
    ones = jnp.ones((width, LANES), BF16)
    norm = jnp.zeros((1, LANES), F32)
    for part, (key_ref, value_ref) in enumerate(((k0_ref, v0_ref), (k1_ref, v1_ref))):
        here = pl.ds(part * keys, keys)
        key = key_ref[...]
        k_ref[here, :] = key
        squares = jnp.dot(key * key, ones, preferred_element_type=F32)
        norm = jnp.maximum(norm, jnp.max(squares, axis=0, keepdims=True))
        v_ref[here, :width] = value_ref[...]
        v_ref[here, width:] = jnp.ones((keys, LANES), BF16)

        @pl.when(valid_ref[part] < keys)
        def _():
            value = v_ref[here, :].astype(F32)
            position = lax.broadcasted_iota(jnp.int32, value.shape, 0)
            v_ref[here, :] = jnp.where(position < valid_ref[part], value, 0.0).astype(BF16)

    scale = TO_BASE_2 / math.sqrt(width)
    norm_ref[...] = jnp.broadcast_to(jnp.sqrt(norm) * (scale * 1.01), norm_ref.shape)


def key_part(valid, k0, k1, v0, v1):
    keys, width = k0.shape
    vmem = pl.BlockSpec(memory_space=pltpu.VMEM)
    smem = pl.BlockSpec(memory_space=pltpu.SMEM)
    return pl.pallas_call(
        key_kernel,
        out_shape=(
            jax.ShapeDtypeStruct((8, LANES), F32),
            jax.ShapeDtypeStruct((2 * keys, width), BF16),
            jax.ShapeDtypeStruct((2 * keys, width + LANES), BF16),
        ),
        in_specs=[smem] + [vmem] * 4,
        out_specs=(vmem,) * 3,
        compiler_params=pltpu.CompilerParams(vmem_limit_bytes=SMALL_VMEM),
        cost_estimate=pl.CostEstimate(
            flops=3 * 10**8, bytes_accessed=4 * 10**6, transcendentals=10**3
        ),
        name="key_part",
    )(valid, k0, k1, v0, v1)


def gate_kernel(k_ref, v_ref, done_ref, k_out, v_out):
    del k_ref, v_ref, done_ref, k_out, v_out


def gate(k, v, done):
    whole = pl.BlockSpec(memory_space=pl.ANY)
    return pl.pallas_call(
        gate_kernel,
        out_shape=(
            jax.ShapeDtypeStruct(k.shape, k.dtype),
            jax.ShapeDtypeStruct(v.shape, v.dtype),
        ),
        in_specs=[whole] * 3,
        out_specs=(whole,) * 2,
        input_output_aliases={0: 0, 1: 1},
        compiler_params=pltpu.CompilerParams(vmem_limit_bytes=SMALL_VMEM),
        name="gate",
    )(k, v, done)


def sent_kernel(length_ref, q_ref, out_ref, rows_ref):
    heads, tokens, width = q_ref.shape
    for h in range(heads):
        rows_ref[pl.ds(h, tokens, stride=heads), :] = q_ref[h].astype(F32)
    out_ref[: heads * tokens, :] = rows_ref[...].astype(BF16)
    length = length_ref[0].astype(F32)
    out_ref[heads * tokens :, :] = jnp.full((TAIL, width), length, F32).astype(BF16)


def sent_rows(length, q):
    heads, tokens, width = q.shape
    return pl.pallas_call(
        sent_kernel,
        out_shape=jax.ShapeDtypeStruct((heads * tokens + TAIL, width), BF16),
        in_specs=[
            pl.BlockSpec(memory_space=pltpu.SMEM),
            pl.BlockSpec(memory_space=pltpu.VMEM),
        ],
        out_specs=pl.BlockSpec(memory_space=pltpu.VMEM),
        scratch_shapes=[pltpu.VMEM((heads * tokens, width), F32)],
        compiler_params=pltpu.CompilerParams(vmem_limit_bytes=SMALL_VMEM),
        name="sent_rows",
    )(length, q)


def own_kernel(heads, q_ref, k_ref, v_ref, mixed_ref, log_ref, column):
    rows, width = mixed_ref.shape
    k = k_ref[...]
    kk = jnp.concatenate([k, k], axis=1)
    s = lax.dot_general(
        scaled_halves(q_ref[:rows, :], TO_BASE_2 / math.sqrt(width)),
        kk,
        NT,
        preferred_element_type=F32,
    )
    row = lax.broadcasted_iota(jnp.int32, s.shape, 0)
    position = lax.broadcasted_iota(jnp.int32, s.shape, 1)
    s = jnp.where(position * heads <= row, s, UNSEEN)
    peak = jnp.max(s, axis=1, keepdims=True)
    weights = jnp.exp2(s - peak)
    weight_sum = jnp.sum(weights, axis=1, keepdims=True)
    mixed_ref[...] = (
        jnp.dot(weights.astype(BF16), v_ref[...], preferred_element_type=F32) / weight_sum
    )
    column[...] = jnp.broadcast_to(jnp.log2(weight_sum) + peak, (rows, LANES))
    for j in range(rows // LANES):
        log_ref[j : j + 1, :] = diagonal_row(column[j * LANES : (j + 1) * LANES, :])


def own_part(heads, q, k, v):
    rows, width = q.shape[0] - TAIL, q.shape[1]
    vmem = pl.BlockSpec(memory_space=pltpu.VMEM)
    return pl.pallas_call(
        functools.partial(own_kernel, heads),
        out_shape=(
            jax.ShapeDtypeStruct((rows, width), F32),
            jax.ShapeDtypeStruct((8, LANES), F32),
        ),
        in_specs=[vmem] * 3,
        out_specs=(vmem,) * 2,
        scratch_shapes=[pltpu.VMEM((rows, LANES), F32)],
        compiler_params=pltpu.CompilerParams(vmem_limit_bytes=SMALL_VMEM),
        cost_estimate=pl.CostEstimate(
            flops=10**8, bytes_accessed=10**6, transcendentals=10**5
        ),
        name="own_part",
    )(q, k, v)


def project_kernel(
    heads, parts_ref, mixed_ref, log_ref, w_hbm, out_ref, w_ref, attended, sems
):
    chunks, _, columns = w_ref.shape
    loads = [
        pltpu.make_async_copy(
            w_hbm.at[:, pl.ds(c * columns, columns)], w_ref.at[c], sems.at[c]
        )
        for c in range(chunks)
    ]
    for load in loads:
        load.start()
    count, rows, width = parts_ref.shape
    rows = rows - TAIL
    lines_each = pl.cdiv(rows, LANES)
    logs = [log_ref[:lines_each, :]]
    for p in range(count):
        tail = parts_ref[p, rows:, :].astype(F32)
        logs.append(
            tail[:lines_each]
            + tail[lines_each : 2 * lines_each]
            + tail[2 * lines_each : 3 * lines_each]
        )
    peak = logs[0]
    for log in logs[1:]:
        peak = jnp.maximum(peak, log)
    shares = [jnp.exp2(log - peak) for log in logs]
    total = shares[0]
    for share in shares[1:]:
        total = total + share
    shares = [share / total for share in shares]
    for j in range(lines_each):
        lines = [share[j : j + 1, :] for share in shares]
        lines.append(jnp.zeros((LANES - len(lines), LANES), F32))
        by_row = jnp.concatenate(lines, axis=0).T
        size = min(LANES, rows - j * LANES)
        here = slice(j * LANES, j * LANES + size)
        value = mixed_ref[here, :] * by_row[:size, 0:1]
        for p in range(count):
            value = value + parts_ref[p, here, :].astype(F32) * by_row[:size, p + 1 : p + 2]
        attended[here, :] = value
    tokens = rows // heads
    wide = jnp.concatenate(
        [attended[pl.ds(h, tokens, stride=heads), :].astype(BF16) for h in range(heads)],
        axis=1,
    )
    for c in range(chunks):
        loads[c].wait()
        out_ref[:, c * columns : (c + 1) * columns] = jnp.dot(
            wide, w_ref[c], preferred_element_type=F32
        ).astype(BF16)


def project(parts, mixed, log, w_out):
    rows, width = mixed.shape
    depth, columns = w_out.shape
    heads = depth // width
    vmem = pl.BlockSpec(memory_space=pltpu.VMEM)
    return pl.pallas_call(
        functools.partial(project_kernel, heads),
        out_shape=jax.ShapeDtypeStruct((rows // heads, columns), BF16),
        in_specs=[vmem] * 3 + [pl.BlockSpec(memory_space=pl.ANY)],
        out_specs=vmem,
        scratch_shapes=[
            pltpu.VMEM((4, depth, columns // 4), BF16),
            pltpu.VMEM(mixed.shape, F32),
            pltpu.SemaphoreType.DMA((4,)),
        ],
        compiler_params=pltpu.CompilerParams(vmem_limit_bytes=PROJECT_VMEM),
        cost_estimate=pl.CostEstimate(
            flops=5 * 10**8, bytes_accessed=10**7, transcendentals=10**5
        ),
        name="project",
    )(parts, mixed, log, w_out)


def per_device(
    queries,
    response_keys,
    response_values,
    prompt_keys,
    prompt_value_rows,
    w_out,
    prompt_len,
    resp_len,
):
    tokens, heads, width = queries.shape[1:]
    rows = tokens * heads
    devices = lax.axis_size("grp")
    me = lax.axis_index("grp")
    ring = devices // NEAR

    def send(x, step, flip):
        route = [
            (i, (i // NEAR + step) % ring * NEAR + (i % NEAR ^ flip)) for i in range(devices)
        ]
        return lax.ppermute(x, "grp", route)

    k_mine = prompt_keys.reshape(-1, width)
    v_mine = prompt_value_rows.reshape(-1, width)
    keys = k_mine.shape[0]
    k_far, v_far = send(k_mine, 0, 2), send(v_mine, 0, 2)
    sent = sent_rows(resp_len, jnp.transpose(queries[0], (1, 0, 2)))
    place = (me // NEAR).astype(jnp.int32)[None]
    gathered = [sent if step == 0 else send(sent, -step, 0) for step in range(ring)]
    k_other, v_other = send(k_mine, 0, 1), send(v_mine, 0, 1)
    mixed, log = own_part(
        heads,
        sent,
        response_keys.reshape(tokens, width),
        response_values.reshape(tokens, width),
    )

    def valid_of(flips):
        begins = jnp.stack([me ^ flip for flip in flips]).astype(jnp.int32) * keys
        return jnp.clip(prompt_len[0] - begins, 0, keys)

    valid = valid_of((0, 1))
    prepared = key_part(valid, k_mine, k_other, v_mine, v_other)
    *state, done = prompt_part(valid, place, gathered, *prepared)
    k_far, v_far = gate(k_far, v_far, done)
    k_last, v_last = send(k_far, 0, 1), send(v_far, 0, 1)
    valid = valid_of((2, 3))
    prepared = key_part(valid, k_far, k_last, v_far, v_last)
    parts = prompt_part(valid, place, gathered, *prepared, state)
    same_place = [[y * NEAR + i for y in range(ring)] for i in range(NEAR)]
    parts = lax.all_to_all(parts, "grp", 0, 0, tiled=True, axis_index_groups=same_place)
    splits = lax.axis_size("head")
    rows_out = tokens // splits
    partial = project(parts, mixed, log, w_out)
    pieces = lax.all_to_all(
        partial.reshape(splits, rows_out, -1), "head", 0, 0, tiled=True
    )
    summed = jnp.sum(pieces.astype(F32), axis=0)
    first_out = lax.axis_index("head") * rows_out
    live_rows = first_out + jnp.arange(rows_out, dtype=jnp.int32) < resp_len[0]
    return jnp.where(live_rows[:, None], summed, 0.0).astype(BF16)[None]


def solution(mesh):
    in_specs = (
        P("grp", None, "head", None),
        P("grp", None, "head", None),
        P("grp", None, "head", None),
        P("grp", "head", None),
        P("grp", "head", None),
        P("head", None),
        P(),
        P("grp"),
    )
    return jax.shard_map(
        per_device,
        mesh=mesh,
        in_specs=in_specs,
        out_specs=P("grp", "head", None),
        check_vma=False,
    )
```

```python
import functools
import math

import jax
import jax.numpy as jnp
from jax import lax
from jax.experimental import pallas as pl
from jax.experimental.pallas import tpu as pltpu
from jax.sharding import PartitionSpec as P

F32, BF16 = jnp.float32, jnp.bfloat16
LANES = 128
BLOCK_ROWS = 512
TAIL = 16
PROMPT_VMEM = 28 * 2**20
SMALL_VMEM = 16 * 2**20
PROJECT_VMEM = 48 * 2**20
NEAR = 4
BATCHES = (((0, 2), (1, 0), (3, 0)), ((1, 2), (3, 2), (2, 0), (2, 2)))
TO_BASE_2 = math.log2(math.e)
UNSEEN = -1e30
NT = (((1,), (1,)), ((), ()))


def scaled_halves(q, scale):
    scaled = q.astype(F32) * scale
    high = scaled.astype(BF16)
    low = (scaled - high.astype(F32)).astype(BF16)
    return jnp.concatenate([high, low], axis=1)


def diagonal_row(tile):
    eye = lax.broadcasted_iota(jnp.int32, tile.shape, 0) == lax.broadcasted_iota(
        jnp.int32, tile.shape, 1
    )
    return jnp.sum(jnp.where(eye, tile, 0.0), axis=0, keepdims=True)


def log_lines(logs, start, count):
    lines = []
    for j in range(count):
        tile = logs[pl.ds(pl.multiple_of(start + j * LANES, 16), LANES), :]
        lines.append(diagonal_row(tile))
    log = jnp.concatenate(lines, axis=0)
    high = log.astype(BF16).astype(F32)
    middle = (log - high).astype(BF16).astype(F32)
    low = log - high - middle
    spare = jnp.zeros((TAIL - 3 * count, LANES), F32)
    return jnp.concatenate([high, middle, low, spare], axis=0).astype(BF16)


def prompt_kernel(responses, valid_ref, *refs):
    q_refs, refs = refs[:responses], refs[responses:]
    norm_ref, k_ref, v_ref = refs[:3]
    out_refs, refs = refs[3 : 3 + responses], refs[3 + responses :]
    packed, mixed, logs, acc = refs
    keys, width = k_ref.shape
    keys = keys // 2
    rows = q_refs[0].shape[0] - TAIL
    heads = rows // LANES
    scale = TO_BASE_2 / math.sqrt(width)
    ones = jnp.ones((16, width), BF16)
    key_norm = norm_ref[0:1, 0:1]

    lengths = [
        jnp.max(q_ref[rows:, :].astype(F32)).astype(jnp.int32) for q_ref in q_refs
    ]
    offset = jnp.int32(0)
    offsets = []
    for i, q_ref in enumerate(q_refs):
        offsets.append(offset)
        packed[pl.ds(pl.multiple_of(offset, 16), rows), :] = q_ref[:rows, :]
        offset = offset + (lengths[i] * heads + 15) // 16 * 16
    total = offset
    packed[pl.ds(pl.multiple_of(offsets[-1], 16) + rows, BLOCK_ROWS), :] = jnp.zeros(
        (BLOCK_ROWS, width), BF16
    )
    valid = (valid_ref[0], valid_ref[1])
    both_valid = jnp.minimum(*valid) > 0
    some_valid = jnp.maximum(*valid) > 0

    def block(b, count):
        here = pl.ds(pl.multiple_of(b * BLOCK_ROWS, BLOCK_ROWS), count)

        def query():
            q = packed[here, :]
            squares = lax.dot_general(ones, q * q, NT, preferred_element_type=F32)
            return scaled_halves(q, scale), jnp.sqrt(squares[:1, :]) * key_norm

        def finish(total, peak):
            weight_sum = total[:, LANES:]
            mixed[here, :] = total[:, :LANES] / weight_sum
            logs[here, :] = jnp.log2(weight_sum) + peak

        def exact():
            halves, _ = query()
            step = 256

            def over_keys(body, carry):
                for part in range(2):

                    def one(c, carry):
                        start = pl.multiple_of(c * step, step)
                        these = pl.ds(pl.multiple_of(part * keys + start, step), step)
                        k = k_ref[these, :]
                        s = lax.dot_general(
                            halves,
                            jnp.concatenate([k, k], axis=1),
                            NT,
                            preferred_element_type=F32,
                        )
                        position = start + lax.broadcasted_iota(jnp.int32, s.shape, 1)
                        s = jnp.where(position < valid[part], s, UNSEEN)
                        return body(s, v_ref[:, these], carry)

                    carry = lax.fori_loop(0, (valid[part] + step - 1) // step, one, carry)
                return carry

            def fold(s, v, peak):
                return jnp.maximum(peak, jnp.max(s, axis=1, keepdims=True))

            peak = over_keys(fold, jnp.full((count, 1), UNSEEN, F32))
            acc[:count, :] = jnp.zeros((count, width + LANES), F32)

            def add(s, v, carry):
                weights = jnp.exp2(s - peak).astype(BF16)
                summed = lax.dot_general(weights, v, NT, preferred_element_type=F32)
                acc[:count, :LANES] += summed[:, :LANES]
                acc[:count, LANES:] += jnp.broadcast_to(
                    summed[:, LANES : LANES + 1], (count, LANES)
                )
                return carry

            over_keys(add, 0)
            finish(acc[:count, :], jnp.broadcast_to(peak, (count, LANES)))

        def quick(start, size):
            halves, bound = query()
            these = pl.ds(start, size)
            k = k_ref[these, :]
            scored = lax.dot_general(
                jnp.concatenate([k, k], axis=1), halves, NT, preferred_element_type=F32
            )
            weights = jnp.exp2(scored - bound).astype(BF16)
            summed = jnp.dot(v_ref[:, these], weights, preferred_element_type=F32)
            weight_sum = summed[LANES : LANES + 1, :]
            total = jnp.concatenate(
                [summed[:LANES].T, jnp.broadcast_to(weight_sum, (LANES, count)).T], axis=1
            )
            finish(total, jnp.broadcast_to(bound, (LANES, count)).T)

            @pl.when(jnp.logical_not(jnp.min(weight_sum) > 2.0**-90))
            def _():
                exact()

        @pl.when(both_valid)
        def _():
            quick(0, 2 * keys)

        @pl.when(jnp.logical_and(some_valid, jnp.logical_not(both_valid)))
        def _():
            quick(pl.multiple_of(jnp.where(valid[0] > 0, 0, keys), keys), keys)

        @pl.when(jnp.logical_not(some_valid))
        def _():
            mixed[here, :] = jnp.zeros((count, width), F32)
            logs[here, :] = jnp.full((count, LANES), UNSEEN, F32)

    half = BLOCK_ROWS // 2
    spare_rows = total % BLOCK_ROWS
    big = total // BLOCK_ROWS + (spare_rows > half).astype(jnp.int32)

    @pl.loop(0, big)
    def _(b):
        block(b, BLOCK_ROWS)

    @pl.when(total > big * BLOCK_ROWS)
    def _():
        block(big, half)

    for i, out_ref in enumerate(out_refs):
        start = pl.multiple_of(offsets[i], 16)
        out_ref[:rows, :] = mixed[pl.ds(start, rows), :].astype(BF16)
        out_ref[rows:, :] = log_lines(logs, start, pl.cdiv(rows, LANES))


def prompt_part(valid, queries, norm, k, v):
    responses = len(queries)
    rows, width = queries[0].shape
    vmem = pl.BlockSpec(memory_space=pltpu.VMEM)
    smem = pl.BlockSpec(memory_space=pltpu.SMEM)
    packed_rows = responses * (rows - TAIL) + BLOCK_ROWS + LANES
    return pl.pallas_call(
        functools.partial(prompt_kernel, responses),
        out_shape=(jax.ShapeDtypeStruct((rows, width), BF16),) * responses,
        in_specs=[smem] + [vmem] * (responses + 3),
        out_specs=(vmem,) * responses,
        scratch_shapes=[
            pltpu.VMEM((packed_rows, width), BF16),
            pltpu.VMEM((packed_rows, width), F32),
            pltpu.VMEM((packed_rows, LANES), F32),
            pltpu.VMEM((BLOCK_ROWS, width + LANES), F32),
        ],
        compiler_params=pltpu.CompilerParams(vmem_limit_bytes=PROMPT_VMEM),
        cost_estimate=pl.CostEstimate(
            flops=10**8, bytes_accessed=10**6, transcendentals=10**5
        ),
        name="prompt_part",
    )(valid, *queries, norm, k, v)


def key_kernel(valid_ref, k0_ref, k1_ref, v0_ref, v1_ref, norm_ref, k_ref, v_ref):
    keys, width = k0_ref.shape
    ones = jnp.ones((width, LANES), BF16)
    norm = jnp.zeros((1, LANES), F32)
    for part, (key_ref, value_ref) in enumerate(((k0_ref, v0_ref), (k1_ref, v1_ref))):
        here = pl.ds(part * keys, keys)
        key = key_ref[...]
        k_ref[here, :] = key
        squares = jnp.dot(key * key, ones, preferred_element_type=F32)
        norm = jnp.maximum(norm, jnp.max(squares, axis=0, keepdims=True))
        v_ref[:width, here] = value_ref[...].T
        v_ref[width:, here] = jnp.ones((TAIL, keys), BF16)

        @pl.when(valid_ref[part] < keys)
        def _():
            value = v_ref[:, here].astype(F32)
            position = lax.broadcasted_iota(jnp.int32, value.shape, 1)
            v_ref[:, here] = jnp.where(position < valid_ref[part], value, 0.0).astype(BF16)

    scale = TO_BASE_2 / math.sqrt(width)
    norm_ref[...] = jnp.broadcast_to(jnp.sqrt(norm) * (scale * 1.01), norm_ref.shape)


def key_part(valid, k0, k1, v0, v1):
    keys, width = k0.shape
    vmem = pl.BlockSpec(memory_space=pltpu.VMEM)
    smem = pl.BlockSpec(memory_space=pltpu.SMEM)
    return pl.pallas_call(
        key_kernel,
        out_shape=(
            jax.ShapeDtypeStruct((8, LANES), F32),
            jax.ShapeDtypeStruct((2 * keys, width), BF16),
            jax.ShapeDtypeStruct((width + TAIL, 2 * keys), BF16),
        ),
        in_specs=[smem] + [vmem] * 4,
        out_specs=(vmem,) * 3,
        compiler_params=pltpu.CompilerParams(vmem_limit_bytes=SMALL_VMEM),
        cost_estimate=pl.CostEstimate(
            flops=3 * 10**8, bytes_accessed=4 * 10**6, transcendentals=10**3
        ),
        name="key_part",
    )(valid, k0, k1, v0, v1)


def sent_kernel(length_ref, q_ref, out_ref, rows_ref):
    heads, tokens, width = q_ref.shape
    for h in range(heads):
        rows_ref[pl.ds(h, tokens, stride=heads), :] = q_ref[h].astype(F32)
    out_ref[: heads * tokens, :] = rows_ref[...].astype(BF16)
    length = length_ref[0].astype(F32)
    out_ref[heads * tokens :, :] = jnp.full((TAIL, width), length, F32).astype(BF16)


def sent_rows(length, q):
    heads, tokens, width = q.shape
    return pl.pallas_call(
        sent_kernel,
        out_shape=jax.ShapeDtypeStruct((heads * tokens + TAIL, width), BF16),
        in_specs=[
            pl.BlockSpec(memory_space=pltpu.SMEM),
            pl.BlockSpec(memory_space=pltpu.VMEM),
        ],
        out_specs=pl.BlockSpec(memory_space=pltpu.VMEM),
        scratch_shapes=[pltpu.VMEM((heads * tokens, width), F32)],
        compiler_params=pltpu.CompilerParams(vmem_limit_bytes=SMALL_VMEM),
        name="sent_rows",
    )(length, q)


def own_kernel(heads, q_ref, k_ref, v_ref, mixed_ref, log_ref, column):
    rows, width = mixed_ref.shape
    k = k_ref[...]
    kk = jnp.concatenate([k, k], axis=1)
    s = lax.dot_general(
        scaled_halves(q_ref[:rows, :], TO_BASE_2 / math.sqrt(width)),
        kk,
        NT,
        preferred_element_type=F32,
    )
    row = lax.broadcasted_iota(jnp.int32, s.shape, 0)
    position = lax.broadcasted_iota(jnp.int32, s.shape, 1)
    s = jnp.where(position * heads <= row, s, UNSEEN)
    peak = jnp.max(s, axis=1, keepdims=True)
    weights = jnp.exp2(s - peak)
    weight_sum = jnp.sum(weights, axis=1, keepdims=True)
    mixed_ref[...] = (
        jnp.dot(weights.astype(BF16), v_ref[...], preferred_element_type=F32) / weight_sum
    )
    column[...] = jnp.broadcast_to(jnp.log2(weight_sum) + peak, (rows, LANES))
    for j in range(rows // LANES):
        log_ref[j : j + 1, :] = diagonal_row(column[j * LANES : (j + 1) * LANES, :])


def own_part(heads, q, k, v):
    rows, width = q.shape[0] - TAIL, q.shape[1]
    vmem = pl.BlockSpec(memory_space=pltpu.VMEM)
    return pl.pallas_call(
        functools.partial(own_kernel, heads),
        out_shape=(
            jax.ShapeDtypeStruct((rows, width), F32),
            jax.ShapeDtypeStruct((8, LANES), F32),
        ),
        in_specs=[vmem] * 3,
        out_specs=(vmem,) * 2,
        scratch_shapes=[pltpu.VMEM((rows, LANES), F32)],
        compiler_params=pltpu.CompilerParams(vmem_limit_bytes=SMALL_VMEM),
        cost_estimate=pl.CostEstimate(
            flops=10**8, bytes_accessed=10**6, transcendentals=10**5
        ),
        name="own_part",
    )(q, k, v)


def project_kernel(
    heads, count, *refs
):
    part_refs = refs[:count]
    mixed_ref, log_ref, w_hbm, out_ref, w_ref, attended, sems = refs[count:]
    chunks, _, columns = w_ref.shape
    loads = [
        pltpu.make_async_copy(
            w_hbm.at[:, pl.ds(c * columns, columns)], w_ref.at[c], sems.at[c]
        )
        for c in range(chunks)
    ]
    for load in loads:
        load.start()
    rows = part_refs[0].shape[0] - TAIL
    lines_each = pl.cdiv(rows, LANES)
    logs = [log_ref[:lines_each, :]]
    for part_ref in part_refs:
        tail = part_ref[rows:, :].astype(F32)
        logs.append(
            tail[:lines_each]
            + tail[lines_each : 2 * lines_each]
            + tail[2 * lines_each : 3 * lines_each]
        )
    peak = logs[0]
    for log in logs[1:]:
        peak = jnp.maximum(peak, log)
    shares = [jnp.exp2(log - peak) for log in logs]
    total = shares[0]
    for share in shares[1:]:
        total = total + share
    shares = [share / total for share in shares]
    for j in range(lines_each):
        lines = [share[j : j + 1, :] for share in shares]
        lines.append(jnp.zeros((LANES - len(lines), LANES), F32))
        by_row = jnp.concatenate(lines, axis=0).T
        size = min(LANES, rows - j * LANES)
        here = slice(j * LANES, j * LANES + size)
        value = mixed_ref[here, :] * by_row[:size, 0:1]
        for p, part_ref in enumerate(part_refs):
            value = value + part_ref[here, :].astype(F32) * by_row[:size, p + 1 : p + 2]
        attended[here, :] = value
    tokens = rows // heads
    wide = jnp.concatenate(
        [attended[pl.ds(h, tokens, stride=heads), :].astype(BF16) for h in range(heads)],
        axis=1,
    )
    for c in range(chunks):
        loads[c].wait()
        out_ref[:, c * columns : (c + 1) * columns] = jnp.dot(
            wide, w_ref[c], preferred_element_type=F32
        ).astype(BF16)


def project(parts, mixed, log, w_out):
    rows, width = mixed.shape
    depth, columns = w_out.shape
    heads = depth // width
    vmem = pl.BlockSpec(memory_space=pltpu.VMEM)
    return pl.pallas_call(
        functools.partial(project_kernel, heads, len(parts)),
        out_shape=jax.ShapeDtypeStruct((rows // heads, columns), BF16),
        in_specs=[vmem] * (len(parts) + 2) + [pl.BlockSpec(memory_space=pl.ANY)],
        out_specs=vmem,
        scratch_shapes=[
            pltpu.VMEM((4, depth, columns // 4), BF16),
            pltpu.VMEM(mixed.shape, F32),
            pltpu.SemaphoreType.DMA((4,)),
        ],
        compiler_params=pltpu.CompilerParams(vmem_limit_bytes=PROJECT_VMEM),
        cost_estimate=pl.CostEstimate(
            flops=5 * 10**8, bytes_accessed=10**7, transcendentals=10**5
        ),
        name="project",
    )(*parts, mixed, log, w_out)


def per_device(
    queries,
    response_keys,
    response_values,
    prompt_keys,
    prompt_value_rows,
    w_out,
    prompt_len,
    resp_len,
):
    tokens, heads, width = queries.shape[1:]
    rows = tokens * heads
    devices = lax.axis_size("grp")
    me = lax.axis_index("grp")
    ring = devices // NEAR

    def send(x, step, flip):
        route = [
            (i, (i // NEAR + step) % ring * NEAR + (i % NEAR ^ flip)) for i in range(devices)
        ]
        return lax.ppermute(x, "grp", route)

    k_mine = prompt_keys.reshape(-1, width)
    v_mine = prompt_value_rows.reshape(-1, width)
    keys = k_mine.shape[0]
    k_other, v_other = send(k_mine, 0, 1), send(v_mine, 0, 1)
    sent = sent_rows(resp_len, jnp.transpose(queries[0], (1, 0, 2)))
    begins = jnp.stack([me, me ^ 1]).astype(jnp.int32) * keys
    valid = jnp.clip(prompt_len[0] - begins, 0, keys)
    prepared = key_part(valid, k_mine, k_other, v_mine, v_other)
    mixed, log = own_part(
        heads,
        sent,
        response_keys.reshape(tokens, width),
        response_values.reshape(tokens, width),
    )
    came = [[send(sent, step, flip) for step, flip in batch] for batch in BATCHES]
    parts = []
    for batch, queries_there in zip(BATCHES, came):
        results = prompt_part(valid, queries_there, *prepared)
        parts += [send(r, -step, flip) for r, (step, flip) in zip(results, batch)]
    parts += prompt_part(valid, [sent], *prepared)
    splits = lax.axis_size("head")
    rows_out = tokens // splits
    partial = project(parts, mixed, log, w_out)
    pieces = lax.all_to_all(
        partial.reshape(splits, rows_out, -1), "head", 0, 0, tiled=True
    )
    summed = jnp.sum(pieces.astype(F32), axis=0)
    first_out = lax.axis_index("head") * rows_out
    live_rows = first_out + jnp.arange(rows_out, dtype=jnp.int32) < resp_len[0]
    return jnp.where(live_rows[:, None], summed, 0.0).astype(BF16)[None]


def solution(mesh):
    in_specs = (
        P("grp", None, "head", None),
        P("grp", None, "head", None),
        P("grp", None, "head", None),
        P("grp", "head", None),
        P("grp", "head", None),
        P("head", None),
        P(),
        P("grp"),
    )
    return jax.shard_map(
        per_device,
        mesh=mesh,
        in_specs=in_specs,
        out_specs=P("grp", "head", None),
        check_vma=False,
    )
```

```python
import functools
import math

import jax
import jax.numpy as jnp
from jax import lax
from jax.experimental import pallas as pl
from jax.experimental.pallas import tpu as pltpu
from jax.sharding import PartitionSpec as P

F32, BF16 = jnp.float32, jnp.bfloat16
LANES = 128
BLOCK_ROWS = 512
TAIL = 16
PROMPT_VMEM = 28 * 2**20
SMALL_VMEM = 16 * 2**20
PROJECT_VMEM = 48 * 2**20
NEAR = 4
BATCHES = (((0, 2), (1, 0), (3, 0)), ((1, 2), (3, 2), (2, 0), (2, 2)))
TO_BASE_2 = math.log2(math.e)
UNSEEN = -1e30
NT = (((1,), (1,)), ((), ()))


def scaled_halves(q, scale):
    scaled = q.astype(F32) * scale
    high = scaled.astype(BF16)
    low = (scaled - high.astype(F32)).astype(BF16)
    return jnp.concatenate([high, low], axis=1)


def diagonal_row(tile):
    eye = lax.broadcasted_iota(jnp.int32, tile.shape, 0) == lax.broadcasted_iota(
        jnp.int32, tile.shape, 1
    )
    return jnp.sum(jnp.where(eye, tile, 0.0), axis=0, keepdims=True)


def log_lines(logs, start, count):
    lines = []
    for j in range(count):
        tile = logs[pl.ds(pl.multiple_of(start + j * LANES, 16), LANES), :]
        lines.append(diagonal_row(tile))
    log = jnp.concatenate(lines, axis=0)
    high = log.astype(BF16).astype(F32)
    middle = (log - high).astype(BF16).astype(F32)
    low = log - high - middle
    spare = jnp.zeros((TAIL - 3 * count, LANES), F32)
    return jnp.concatenate([high, middle, low, spare], axis=0).astype(BF16)


def prompt_kernel(responses, valid_ref, *refs):
    q_refs, refs = refs[:responses], refs[responses:]
    norm_ref, k_ref, v_ref = refs[:3]
    out_refs, refs = refs[3 : 3 + responses], refs[3 + responses :]
    packed, mixed, logs, acc, lowest = refs
    keys, width = k_ref.shape
    keys = keys // 2
    rows = q_refs[0].shape[0] - TAIL
    heads = rows // LANES
    scale = TO_BASE_2 / math.sqrt(width)
    ones = jnp.ones((16, width), BF16)
    key_norm = norm_ref[0:1, 0:1]

    lengths = [
        jnp.max(q_ref[rows:, :].astype(F32)).astype(jnp.int32) for q_ref in q_refs
    ]
    offset = jnp.int32(0)
    offsets = []
    for i, q_ref in enumerate(q_refs):
        offsets.append(offset)
        packed[pl.ds(pl.multiple_of(offset, 16), rows), :] = q_ref[:rows, :]
        offset = offset + (lengths[i] * heads + 15) // 16 * 16
    total = offset
    packed[pl.ds(pl.multiple_of(offsets[-1], 16) + rows, BLOCK_ROWS), :] = jnp.zeros(
        (BLOCK_ROWS, width), BF16
    )
    valid = (valid_ref[0], valid_ref[1])
    some_valid = jnp.maximum(*valid) > 0
    lowest[...] = jnp.ones_like(lowest)

    def finish(here, total, peak):
        weight_sum = total[:, LANES:]
        mixed[here, :] = total[:, :LANES] / weight_sum
        logs[here, :] = jnp.log2(weight_sum) + peak

    def block(first, count):
        here = pl.ds(first, count)

        @pl.when(some_valid)
        def _():
            q = packed[here, :]
            squares = lax.dot_general(ones, q * q, NT, preferred_element_type=F32)
            bound = jnp.sqrt(squares[:1, :]) * key_norm
            k = k_ref[...]
            scored = lax.dot_general(
                jnp.concatenate([k, k], axis=1),
                scaled_halves(q, scale),
                NT,
                preferred_element_type=F32,
            )
            weights = jnp.exp2(scored - bound).astype(BF16)
            summed = jnp.dot(v_ref[...], weights, preferred_element_type=F32)
            weight_sum = summed[LANES : LANES + 1, :]
            lowest[:, :count] = jnp.minimum(lowest[:, :count], weight_sum)
            total = jnp.concatenate(
                [summed[:LANES].T, jnp.broadcast_to(weight_sum, (LANES, count)).T], axis=1
            )
            finish(here, total, jnp.broadcast_to(bound, (LANES, count)).T)

        @pl.when(jnp.logical_not(some_valid))
        def _():
            mixed[here, :] = jnp.zeros((count, width), F32)
            logs[here, :] = jnp.full((count, LANES), UNSEEN, F32)

    def exact_block(first, count):
        here = pl.ds(first, count)
        halves = scaled_halves(packed[here, :], scale)
        step = 256

        def over_keys(body, carry):
            def one(c, carry):
                start = pl.multiple_of(c * step, step)
                these = pl.ds(start, step)
                k = k_ref[these, :]
                s = lax.dot_general(
                    halves,
                    jnp.concatenate([k, k], axis=1),
                    NT,
                    preferred_element_type=F32,
                )
                second = start >= keys
                position = lax.broadcasted_iota(jnp.int32, s.shape, 1)
                position = position + (start - jnp.where(second, keys, 0))
                s = jnp.where(position < jnp.where(second, valid[1], valid[0]), s, UNSEEN)
                return body(s, v_ref[:, these], carry)

            return lax.fori_loop(0, 2 * keys // step, one, carry)

        def fold(s, v, peak):
            return jnp.maximum(peak, jnp.max(s, axis=1, keepdims=True))

        peak = over_keys(fold, jnp.full((count, 1), UNSEEN, F32))
        acc[...] = jnp.zeros_like(acc)

        def add(s, v, carry):
            weights = jnp.exp2(s - peak).astype(BF16)
            summed = lax.dot_general(weights, v, NT, preferred_element_type=F32)
            acc[:, :LANES] += summed[:, :LANES]
            acc[:, LANES:] += jnp.broadcast_to(
                summed[:, LANES : LANES + 1], (count, LANES)
            )
            return carry

        over_keys(add, 0)
        finish(here, acc[...], jnp.broadcast_to(peak, (count, LANES)))

    half = BLOCK_ROWS // 2
    spare_rows = total % BLOCK_ROWS
    big = total // BLOCK_ROWS + (spare_rows > half).astype(jnp.int32)

    @pl.loop(0, big)
    def _(b):
        block(pl.multiple_of(b * BLOCK_ROWS, BLOCK_ROWS), BLOCK_ROWS)

    @pl.when(total > big * BLOCK_ROWS)
    def _():
        block(pl.multiple_of(big * BLOCK_ROWS, BLOCK_ROWS), half)

    @pl.when(jnp.logical_and(some_valid, jnp.logical_not(jnp.min(lowest[...]) > 2.0**-90)))
    def _():
        @pl.loop(0, (total + half - 1) // half)
        def _(b):
            exact_block(pl.multiple_of(b * half, half), half)

    for i, out_ref in enumerate(out_refs):
        start = pl.multiple_of(offsets[i], 16)
        out_ref[:rows, :] = mixed[pl.ds(start, rows), :].astype(BF16)
        out_ref[rows:, :] = log_lines(logs, start, pl.cdiv(rows, LANES))


def prompt_part(valid, queries, norm, k, v):
    responses = len(queries)
    rows, width = queries[0].shape
    vmem = pl.BlockSpec(memory_space=pltpu.VMEM)
    smem = pl.BlockSpec(memory_space=pltpu.SMEM)
    packed_rows = responses * (rows - TAIL) + BLOCK_ROWS + LANES
    return pl.pallas_call(
        functools.partial(prompt_kernel, responses),
        out_shape=(jax.ShapeDtypeStruct((rows, width), BF16),) * responses,
        in_specs=[smem] + [vmem] * (responses + 3),
        out_specs=(vmem,) * responses,
        scratch_shapes=[
            pltpu.VMEM((packed_rows, width), BF16),
            pltpu.VMEM((packed_rows, width), F32),
            pltpu.VMEM((packed_rows, LANES), F32),
            pltpu.VMEM((BLOCK_ROWS // 2, width + LANES), F32),
            pltpu.VMEM((1, BLOCK_ROWS), F32),
        ],
        compiler_params=pltpu.CompilerParams(vmem_limit_bytes=PROMPT_VMEM),
        cost_estimate=pl.CostEstimate(
            flops=10**8, bytes_accessed=10**6, transcendentals=10**5
        ),
        name="prompt_part",
    )(valid, *queries, norm, k, v)


def key_kernel(valid_ref, k0_ref, k1_ref, v0_ref, v1_ref, norm_ref, k_ref, v_ref):
    keys, width = k0_ref.shape
    ones = jnp.ones((width, LANES), BF16)
    norm = jnp.zeros((1, LANES), F32)
    for part, (key_ref, value_ref) in enumerate(((k0_ref, v0_ref), (k1_ref, v1_ref))):
        here = pl.ds(part * keys, keys)
        key = key_ref[...]
        k_ref[here, :] = key
        squares = jnp.dot(key * key, ones, preferred_element_type=F32)
        norm = jnp.maximum(norm, jnp.max(squares, axis=0, keepdims=True))
        v_ref[:width, here] = value_ref[...].T
        v_ref[width:, here] = jnp.ones((TAIL, keys), BF16)

        @pl.when(valid_ref[part] < keys)
        def _():
            value = v_ref[:, here].astype(F32)
            position = lax.broadcasted_iota(jnp.int32, value.shape, 1)
            v_ref[:, here] = jnp.where(position < valid_ref[part], value, 0.0).astype(BF16)

    scale = TO_BASE_2 / math.sqrt(width)
    norm_ref[...] = jnp.broadcast_to(jnp.sqrt(norm) * (scale * 1.01), norm_ref.shape)


def key_part(valid, k0, k1, v0, v1):
    keys, width = k0.shape
    vmem = pl.BlockSpec(memory_space=pltpu.VMEM)
    smem = pl.BlockSpec(memory_space=pltpu.SMEM)
    return pl.pallas_call(
        key_kernel,
        out_shape=(
            jax.ShapeDtypeStruct((8, LANES), F32),
            jax.ShapeDtypeStruct((2 * keys, width), BF16),
            jax.ShapeDtypeStruct((width + TAIL, 2 * keys), BF16),
        ),
        in_specs=[smem] + [vmem] * 4,
        out_specs=(vmem,) * 3,
        compiler_params=pltpu.CompilerParams(vmem_limit_bytes=SMALL_VMEM),
        cost_estimate=pl.CostEstimate(
            flops=3 * 10**8, bytes_accessed=4 * 10**6, transcendentals=10**3
        ),
        name="key_part",
    )(valid, k0, k1, v0, v1)


def sent_kernel(length_ref, q_ref, out_ref, rows_ref):
    heads, tokens, width = q_ref.shape
    for h in range(heads):
        rows_ref[pl.ds(h, tokens, stride=heads), :] = q_ref[h].astype(F32)
    out_ref[: heads * tokens, :] = rows_ref[...].astype(BF16)
    length = length_ref[0].astype(F32)
    out_ref[heads * tokens :, :] = jnp.full((TAIL, width), length, F32).astype(BF16)


def sent_rows(length, q):
    heads, tokens, width = q.shape
    return pl.pallas_call(
        sent_kernel,
        out_shape=jax.ShapeDtypeStruct((heads * tokens + TAIL, width), BF16),
        in_specs=[
            pl.BlockSpec(memory_space=pltpu.SMEM),
            pl.BlockSpec(memory_space=pltpu.VMEM),
        ],
        out_specs=pl.BlockSpec(memory_space=pltpu.VMEM),
        scratch_shapes=[pltpu.VMEM((heads * tokens, width), F32)],
        compiler_params=pltpu.CompilerParams(vmem_limit_bytes=SMALL_VMEM),
        name="sent_rows",
    )(length, q)


def own_kernel(heads, q_ref, k_ref, v_ref, mixed_ref, log_ref, column):
    rows, width = mixed_ref.shape
    k = k_ref[...]
    kk = jnp.concatenate([k, k], axis=1)
    s = lax.dot_general(
        scaled_halves(q_ref[:rows, :], TO_BASE_2 / math.sqrt(width)),
        kk,
        NT,
        preferred_element_type=F32,
    )
    row = lax.broadcasted_iota(jnp.int32, s.shape, 0)
    position = lax.broadcasted_iota(jnp.int32, s.shape, 1)
    s = jnp.where(position * heads <= row, s, UNSEEN)
    peak = jnp.max(s, axis=1, keepdims=True)
    weights = jnp.exp2(s - peak)
    weight_sum = jnp.sum(weights, axis=1, keepdims=True)
    mixed_ref[...] = (
        jnp.dot(weights.astype(BF16), v_ref[...], preferred_element_type=F32) / weight_sum
    )
    column[...] = jnp.broadcast_to(jnp.log2(weight_sum) + peak, (rows, LANES))
    for j in range(rows // LANES):
        log_ref[j : j + 1, :] = diagonal_row(column[j * LANES : (j + 1) * LANES, :])


def own_part(heads, q, k, v):
    rows, width = q.shape[0] - TAIL, q.shape[1]
    vmem = pl.BlockSpec(memory_space=pltpu.VMEM)
    return pl.pallas_call(
        functools.partial(own_kernel, heads),
        out_shape=(
            jax.ShapeDtypeStruct((rows, width), F32),
            jax.ShapeDtypeStruct((8, LANES), F32),
        ),
        in_specs=[vmem] * 3,
        out_specs=(vmem,) * 2,
        scratch_shapes=[pltpu.VMEM((rows, LANES), F32)],
        compiler_params=pltpu.CompilerParams(vmem_limit_bytes=SMALL_VMEM),
        cost_estimate=pl.CostEstimate(
            flops=10**8, bytes_accessed=10**6, transcendentals=10**5
        ),
        name="own_part",
    )(q, k, v)


def project_kernel(
    heads, count, *refs
):
    part_refs = refs[:count]
    mixed_ref, log_ref, w_hbm, out_ref, w_ref, attended, sems = refs[count:]
    chunks, _, columns = w_ref.shape
    loads = [
        pltpu.make_async_copy(
            w_hbm.at[:, pl.ds(c * columns, columns)], w_ref.at[c], sems.at[c]
        )
        for c in range(chunks)
    ]
    for load in loads:
        load.start()
    rows = part_refs[0].shape[0] - TAIL
    lines_each = pl.cdiv(rows, LANES)
    logs = [log_ref[:lines_each, :]]
    for part_ref in part_refs:
        tail = part_ref[rows:, :].astype(F32)
        logs.append(
            tail[:lines_each]
            + tail[lines_each : 2 * lines_each]
            + tail[2 * lines_each : 3 * lines_each]
        )
    peak = logs[0]
    for log in logs[1:]:
        peak = jnp.maximum(peak, log)
    shares = [jnp.exp2(log - peak) for log in logs]
    total = shares[0]
    for share in shares[1:]:
        total = total + share
    shares = [share / total for share in shares]
    for j in range(lines_each):
        lines = [share[j : j + 1, :] for share in shares]
        lines.append(jnp.zeros((LANES - len(lines), LANES), F32))
        by_row = jnp.concatenate(lines, axis=0).T
        size = min(LANES, rows - j * LANES)
        here = slice(j * LANES, j * LANES + size)
        value = mixed_ref[here, :] * by_row[:size, 0:1]
        for p, part_ref in enumerate(part_refs):
            value = value + part_ref[here, :].astype(F32) * by_row[:size, p + 1 : p + 2]
        attended[here, :] = value
    tokens = rows // heads
    wide = jnp.concatenate(
        [attended[pl.ds(h, tokens, stride=heads), :].astype(BF16) for h in range(heads)],
        axis=1,
    )
    for c in range(chunks):
        loads[c].wait()
        out_ref[:, c * columns : (c + 1) * columns] = jnp.dot(
            wide, w_ref[c], preferred_element_type=F32
        ).astype(BF16)


def project(parts, mixed, log, w_out):
    rows, width = mixed.shape
    depth, columns = w_out.shape
    heads = depth // width
    vmem = pl.BlockSpec(memory_space=pltpu.VMEM)
    return pl.pallas_call(
        functools.partial(project_kernel, heads, len(parts)),
        out_shape=jax.ShapeDtypeStruct((rows // heads, columns), BF16),
        in_specs=[vmem] * (len(parts) + 2) + [pl.BlockSpec(memory_space=pl.ANY)],
        out_specs=vmem,
        scratch_shapes=[
            pltpu.VMEM((4, depth, columns // 4), BF16),
            pltpu.VMEM(mixed.shape, F32),
            pltpu.SemaphoreType.DMA((4,)),
        ],
        compiler_params=pltpu.CompilerParams(vmem_limit_bytes=PROJECT_VMEM),
        cost_estimate=pl.CostEstimate(
            flops=5 * 10**8, bytes_accessed=10**7, transcendentals=10**5
        ),
        name="project",
    )(*parts, mixed, log, w_out)


def per_device(
    queries,
    response_keys,
    response_values,
    prompt_keys,
    prompt_value_rows,
    w_out,
    prompt_len,
    resp_len,
):
    tokens, heads, width = queries.shape[1:]
    rows = tokens * heads
    devices = lax.axis_size("grp")
    me = lax.axis_index("grp")
    ring = devices // NEAR

    def send(x, step, flip):
        route = [
            (i, (i // NEAR + step) % ring * NEAR + (i % NEAR ^ flip)) for i in range(devices)
        ]
        return lax.ppermute(x, "grp", route)

    k_mine = prompt_keys.reshape(-1, width)
    v_mine = prompt_value_rows.reshape(-1, width)
    keys = k_mine.shape[0]
    k_other, v_other = send(k_mine, 0, 1), send(v_mine, 0, 1)
    sent = sent_rows(resp_len, jnp.transpose(queries[0], (1, 0, 2)))
    begins = jnp.stack([me, me ^ 1]).astype(jnp.int32) * keys
    valid = jnp.clip(prompt_len[0] - begins, 0, keys)
    prepared = key_part(valid, k_mine, k_other, v_mine, v_other)
    mixed, log = own_part(
        heads,
        sent,
        response_keys.reshape(tokens, width),
        response_values.reshape(tokens, width),
    )
    came = [[send(sent, step, flip) for step, flip in batch] for batch in BATCHES]
    parts = []
    for batch, queries_there in zip(BATCHES, came):
        results = prompt_part(valid, queries_there, *prepared)
        parts += [send(r, -step, flip) for r, (step, flip) in zip(results, batch)]
    parts += prompt_part(valid, [sent], *prepared)
    splits = lax.axis_size("head")
    rows_out = tokens // splits
    partial = project(parts, mixed, log, w_out)
    pieces = lax.all_to_all(
        partial.reshape(splits, rows_out, -1), "head", 0, 0, tiled=True
    )
    summed = jnp.sum(pieces.astype(F32), axis=0)
    first_out = lax.axis_index("head") * rows_out
    live_rows = first_out + jnp.arange(rows_out, dtype=jnp.int32) < resp_len[0]
    return jnp.where(live_rows[:, None], summed, 0.0).astype(BF16)[None]


def solution(mesh):
    in_specs = (
        P("grp", None, "head", None),
        P("grp", None, "head", None),
        P("grp", None, "head", None),
        P("grp", "head", None),
        P("grp", "head", None),
        P("head", None),
        P(),
        P("grp"),
    )
    return jax.shard_map(
        per_device,
        mesh=mesh,
        in_specs=in_specs,
        out_specs=P("grp", "head", None),
        check_vma=False,
    )
```

```python
import functools
import math

import jax
import jax.numpy as jnp
from jax import lax
from jax.experimental import pallas as pl
from jax.experimental.pallas import tpu as pltpu
from jax.sharding import PartitionSpec as P

F32, BF16 = jnp.float32, jnp.bfloat16
LANES = 128
BLOCK_ROWS = 512
TAIL = 16
PROMPT_VMEM = 28 * 2**20
SMALL_VMEM = 16 * 2**20
PROJECT_VMEM = 48 * 2**20
NEAR = 4
BATCHES = (((0, 2), (1, 0), (3, 0)), ((1, 2), (3, 2), (2, 0), (2, 2)))
TO_BASE_2 = math.log2(math.e)
UNSEEN = -1e30
NT = (((1,), (1,)), ((), ()))


def scaled_halves(q, scale):
    scaled = q.astype(F32) * scale
    high = scaled.astype(BF16)
    low = (scaled - high.astype(F32)).astype(BF16)
    return jnp.concatenate([high, low], axis=1)


def diagonal_row(tile):
    eye = lax.broadcasted_iota(jnp.int32, tile.shape, 0) == lax.broadcasted_iota(
        jnp.int32, tile.shape, 1
    )
    return jnp.sum(jnp.where(eye, tile, 0.0), axis=0, keepdims=True)


def log_lines(logs, start, count):
    lines = []
    for j in range(count):
        tile = logs[pl.ds(pl.multiple_of(start + j * LANES, 16), LANES), :]
        lines.append(diagonal_row(tile))
    log = jnp.concatenate(lines, axis=0)
    high = log.astype(BF16).astype(F32)
    middle = (log - high).astype(BF16).astype(F32)
    low = log - high - middle
    spare = jnp.zeros((TAIL - 3 * count, LANES), F32)
    return jnp.concatenate([high, middle, low, spare], axis=0).astype(BF16)


def prompt_kernel(responses, valid_ref, *refs):
    q_refs, refs = refs[:responses], refs[responses:]
    norm_ref, k_ref, v_ref = refs[:3]
    out_refs, refs = refs[3 : 3 + responses], refs[3 + responses :]
    packed, mixed, logs, acc, lowest = refs
    keys, width = k_ref.shape
    keys = keys // 2
    rows = q_refs[0].shape[0] - TAIL
    heads = rows // LANES
    scale = TO_BASE_2 / math.sqrt(width)
    ones = jnp.ones((16, width), BF16)
    key_norm = norm_ref[0:1, 0:1]

    lengths = [
        jnp.max(q_ref[rows:, :].astype(F32)).astype(jnp.int32) for q_ref in q_refs
    ]
    offset = jnp.int32(0)
    offsets = []
    for i, q_ref in enumerate(q_refs):
        offsets.append(offset)
        packed[pl.ds(pl.multiple_of(offset, 16), rows), :] = q_ref[:rows, :]
        offset = offset + (lengths[i] * heads + 15) // 16 * 16
    total = offset
    packed[pl.ds(pl.multiple_of(offsets[-1], 16) + rows, BLOCK_ROWS), :] = jnp.zeros(
        (BLOCK_ROWS, width), BF16
    )
    valid = (valid_ref[0], valid_ref[1])
    some_valid = jnp.maximum(*valid) > 0
    lowest[...] = jnp.ones_like(lowest)

    def block(first, count):
        here = pl.ds(first, count)

        @pl.when(some_valid)
        def _():
            q = packed[here, :]
            squares = lax.dot_general(ones, q * q, NT, preferred_element_type=F32)
            bound = jnp.sqrt(squares[:1, :]) * key_norm
            k = k_ref[...]
            scored = lax.dot_general(
                jnp.concatenate([k, k], axis=1),
                scaled_halves(q, scale),
                NT,
                preferred_element_type=F32,
            )
            weights = jnp.exp2(scored - bound).astype(BF16)
            summed = jnp.dot(v_ref[...], weights, preferred_element_type=F32)
            weight_sum = summed[LANES : LANES + 1, :]
            lowest[:, :count] = jnp.minimum(lowest[:, :count], weight_sum)
            log = jnp.log2(weight_sum) + bound
            mixed[here, :] = (summed[:LANES] * (1.0 / weight_sum)).T
            logs[here, :] = jnp.broadcast_to(log, (LANES, count)).T

        @pl.when(jnp.logical_not(some_valid))
        def _():
            mixed[here, :] = jnp.zeros((count, width), F32)
            logs[here, :] = jnp.full((count, LANES), UNSEEN, F32)

    def exact_block(first, count):
        here = pl.ds(first, count)
        halves = scaled_halves(packed[here, :], scale)
        step = 256

        def over_keys(body, carry):
            def one(c, carry):
                start = pl.multiple_of(c * step, step)
                these = pl.ds(start, step)
                k = k_ref[these, :]
                s = lax.dot_general(
                    halves,
                    jnp.concatenate([k, k], axis=1),
                    NT,
                    preferred_element_type=F32,
                )
                second = start >= keys
                position = lax.broadcasted_iota(jnp.int32, s.shape, 1)
                position = position + (start - jnp.where(second, keys, 0))
                s = jnp.where(position < jnp.where(second, valid[1], valid[0]), s, UNSEEN)
                return body(s, v_ref[:, these], carry)

            return lax.fori_loop(0, 2 * keys // step, one, carry)

        def fold(s, v, peak):
            return jnp.maximum(peak, jnp.max(s, axis=1, keepdims=True))

        peak = over_keys(fold, jnp.full((count, 1), UNSEEN, F32))
        acc[...] = jnp.zeros_like(acc)

        def add(s, v, carry):
            weights = jnp.exp2(s - peak).astype(BF16)
            summed = lax.dot_general(weights, v, NT, preferred_element_type=F32)
            acc[:, :LANES] += summed[:, :LANES]
            acc[:, LANES:] += jnp.broadcast_to(
                summed[:, LANES : LANES + 1], (count, LANES)
            )
            return carry

        over_keys(add, 0)
        weight_sum = acc[:, LANES:]
        mixed[here, :] = acc[:, :LANES] / weight_sum
        logs[here, :] = jnp.log2(weight_sum) + jnp.broadcast_to(peak, (count, LANES))

    half = BLOCK_ROWS // 2
    spare_rows = total % BLOCK_ROWS
    big = total // BLOCK_ROWS + (spare_rows > half).astype(jnp.int32)

    @pl.loop(0, big)
    def _(b):
        block(pl.multiple_of(b * BLOCK_ROWS, BLOCK_ROWS), BLOCK_ROWS)

    @pl.when(total > big * BLOCK_ROWS)
    def _():
        block(pl.multiple_of(big * BLOCK_ROWS, BLOCK_ROWS), half)

    @pl.when(jnp.logical_and(some_valid, jnp.logical_not(jnp.min(lowest[...]) > 2.0**-90)))
    def _():
        @pl.loop(0, (total + half - 1) // half)
        def _(b):
            exact_block(pl.multiple_of(b * half, half), half)

    for i, out_ref in enumerate(out_refs):
        start = pl.multiple_of(offsets[i], 16)
        out_ref[:rows, :] = mixed[pl.ds(start, rows), :].astype(BF16)
        out_ref[rows:, :] = log_lines(logs, start, pl.cdiv(rows, LANES))


def prompt_part(valid, queries, norm, k, v):
    responses = len(queries)
    rows, width = queries[0].shape
    vmem = pl.BlockSpec(memory_space=pltpu.VMEM)
    smem = pl.BlockSpec(memory_space=pltpu.SMEM)
    packed_rows = responses * (rows - TAIL) + BLOCK_ROWS + LANES
    return pl.pallas_call(
        functools.partial(prompt_kernel, responses),
        out_shape=(jax.ShapeDtypeStruct((rows, width), BF16),) * responses,
        in_specs=[smem] + [vmem] * (responses + 3),
        out_specs=(vmem,) * responses,
        scratch_shapes=[
            pltpu.VMEM((packed_rows, width), BF16),
            pltpu.VMEM((packed_rows, width), F32),
            pltpu.VMEM((packed_rows, LANES), F32),
            pltpu.VMEM((BLOCK_ROWS // 2, width + LANES), F32),
            pltpu.VMEM((1, BLOCK_ROWS), F32),
        ],
        compiler_params=pltpu.CompilerParams(vmem_limit_bytes=PROMPT_VMEM),
        cost_estimate=pl.CostEstimate(
            flops=10**8, bytes_accessed=10**6, transcendentals=10**5
        ),
        name="prompt_part",
    )(valid, *queries, norm, k, v)


def key_kernel(valid_ref, k0_ref, k1_ref, v0_ref, v1_ref, norm_ref, k_ref, v_ref):
    keys, width = k0_ref.shape
    ones = jnp.ones((width, LANES), BF16)
    norm = jnp.zeros((1, LANES), F32)
    for part, (key_ref, value_ref) in enumerate(((k0_ref, v0_ref), (k1_ref, v1_ref))):
        here = pl.ds(part * keys, keys)
        key = key_ref[...]
        k_ref[here, :] = key
        squares = jnp.dot(key * key, ones, preferred_element_type=F32)
        norm = jnp.maximum(norm, jnp.max(squares, axis=0, keepdims=True))
        v_ref[:width, here] = value_ref[...].T
        v_ref[width:, here] = jnp.ones((TAIL, keys), BF16)

        @pl.when(valid_ref[part] < keys)
        def _():
            value = v_ref[:, here].astype(F32)
            position = lax.broadcasted_iota(jnp.int32, value.shape, 1)
            v_ref[:, here] = jnp.where(position < valid_ref[part], value, 0.0).astype(BF16)

    scale = TO_BASE_2 / math.sqrt(width)
    norm_ref[...] = jnp.broadcast_to(jnp.sqrt(norm) * (scale * 1.01), norm_ref.shape)


def key_part(valid, k0, k1, v0, v1):
    keys, width = k0.shape
    vmem = pl.BlockSpec(memory_space=pltpu.VMEM)
    smem = pl.BlockSpec(memory_space=pltpu.SMEM)
    return pl.pallas_call(
        key_kernel,
        out_shape=(
            jax.ShapeDtypeStruct((8, LANES), F32),
            jax.ShapeDtypeStruct((2 * keys, width), BF16),
            jax.ShapeDtypeStruct((width + TAIL, 2 * keys), BF16),
        ),
        in_specs=[smem] + [vmem] * 4,
        out_specs=(vmem,) * 3,
        compiler_params=pltpu.CompilerParams(vmem_limit_bytes=SMALL_VMEM),
        cost_estimate=pl.CostEstimate(
            flops=3 * 10**8, bytes_accessed=4 * 10**6, transcendentals=10**3
        ),
        name="key_part",
    )(valid, k0, k1, v0, v1)


def sent_kernel(length_ref, q_ref, out_ref, rows_ref):
    heads, tokens, width = q_ref.shape
    for h in range(heads):
        rows_ref[pl.ds(h, tokens, stride=heads), :] = q_ref[h].astype(F32)
    out_ref[: heads * tokens, :] = rows_ref[...].astype(BF16)
    length = length_ref[0].astype(F32)
    out_ref[heads * tokens :, :] = jnp.full((TAIL, width), length, F32).astype(BF16)


def sent_rows(length, q):
    heads, tokens, width = q.shape
    return pl.pallas_call(
        sent_kernel,
        out_shape=jax.ShapeDtypeStruct((heads * tokens + TAIL, width), BF16),
        in_specs=[
            pl.BlockSpec(memory_space=pltpu.SMEM),
            pl.BlockSpec(memory_space=pltpu.VMEM),
        ],
        out_specs=pl.BlockSpec(memory_space=pltpu.VMEM),
        scratch_shapes=[pltpu.VMEM((heads * tokens, width), F32)],
        compiler_params=pltpu.CompilerParams(vmem_limit_bytes=SMALL_VMEM),
        name="sent_rows",
    )(length, q)


def own_kernel(heads, q_ref, k_ref, v_ref, mixed_ref, log_ref, column):
    rows, width = mixed_ref.shape
    k = k_ref[...]
    kk = jnp.concatenate([k, k], axis=1)
    s = lax.dot_general(
        scaled_halves(q_ref[:rows, :], TO_BASE_2 / math.sqrt(width)),
        kk,
        NT,
        preferred_element_type=F32,
    )
    row = lax.broadcasted_iota(jnp.int32, s.shape, 0)
    position = lax.broadcasted_iota(jnp.int32, s.shape, 1)
    s = jnp.where(position * heads <= row, s, UNSEEN)
    peak = jnp.max(s, axis=1, keepdims=True)
    weights = jnp.exp2(s - peak)
    weight_sum = jnp.sum(weights, axis=1, keepdims=True)
    mixed_ref[...] = (
        jnp.dot(weights.astype(BF16), v_ref[...], preferred_element_type=F32) / weight_sum
    )
    column[...] = jnp.broadcast_to(jnp.log2(weight_sum) + peak, (rows, LANES))
    for j in range(rows // LANES):
        log_ref[j : j + 1, :] = diagonal_row(column[j * LANES : (j + 1) * LANES, :])


def own_part(heads, q, k, v):
    rows, width = q.shape[0] - TAIL, q.shape[1]
    vmem = pl.BlockSpec(memory_space=pltpu.VMEM)
    return pl.pallas_call(
        functools.partial(own_kernel, heads),
        out_shape=(
            jax.ShapeDtypeStruct((rows, width), F32),
            jax.ShapeDtypeStruct((8, LANES), F32),
        ),
        in_specs=[vmem] * 3,
        out_specs=(vmem,) * 2,
        scratch_shapes=[pltpu.VMEM((rows, LANES), F32)],
        compiler_params=pltpu.CompilerParams(vmem_limit_bytes=SMALL_VMEM),
        cost_estimate=pl.CostEstimate(
            flops=10**8, bytes_accessed=10**6, transcendentals=10**5
        ),
        name="own_part",
    )(q, k, v)


def project_kernel(
    heads, count, *refs
):
    part_refs = refs[:count]
    mixed_ref, log_ref, w_hbm, out_ref, w_ref, attended, sems = refs[count:]
    chunks, _, columns = w_ref.shape
    loads = [
        pltpu.make_async_copy(
            w_hbm.at[:, pl.ds(c * columns, columns)], w_ref.at[c], sems.at[c]
        )
        for c in range(chunks)
    ]
    for load in loads:
        load.start()
    rows = part_refs[0].shape[0] - TAIL
    lines_each = pl.cdiv(rows, LANES)
    logs = [log_ref[:lines_each, :]]
    for part_ref in part_refs:
        tail = part_ref[rows:, :].astype(F32)
        logs.append(
            tail[:lines_each]
            + tail[lines_each : 2 * lines_each]
            + tail[2 * lines_each : 3 * lines_each]
        )
    peak = logs[0]
    for log in logs[1:]:
        peak = jnp.maximum(peak, log)
    shares = [jnp.exp2(log - peak) for log in logs]
    total = shares[0]
    for share in shares[1:]:
        total = total + share
    shares = [share / total for share in shares]
    spread_shape = (2 * LANES, len(shares) * LANES)
    spread = jnp.where(
        lax.broadcasted_iota(jnp.int32, spread_shape, 0) % LANES
        == lax.broadcasted_iota(jnp.int32, spread_shape, 1) // LANES,
        1.0,
        0.0,
    ).astype(BF16)
    for j in range(lines_each):
        lines = [share[j : j + 1, :] for share in shares]
        lines.append(jnp.zeros((LANES - len(lines), LANES), F32))
        by_row = jnp.concatenate(lines, axis=0).T
        size = min(LANES, rows - j * LANES)
        here = slice(j * LANES, j * LANES + size)
        by_row = jnp.dot(scaled_halves(by_row, 1.0), spread, preferred_element_type=F32)
        value = mixed_ref[here, :] * by_row[:size, :LANES]
        for p, part_ref in enumerate(part_refs):
            share = by_row[:size, (p + 1) * LANES : (p + 2) * LANES]
            value = value + part_ref[here, :].astype(F32) * share
        attended[here, :] = value
    tokens = rows // heads
    wide = jnp.concatenate(
        [attended[pl.ds(h, tokens, stride=heads), :].astype(BF16) for h in range(heads)],
        axis=1,
    )
    for c in range(chunks):
        loads[c].wait()
        out_ref[:, c * columns : (c + 1) * columns] = jnp.dot(
            wide, w_ref[c], preferred_element_type=F32
        ).astype(BF16)


def project(parts, mixed, log, w_out):
    rows, width = mixed.shape
    depth, columns = w_out.shape
    heads = depth // width
    vmem = pl.BlockSpec(memory_space=pltpu.VMEM)
    return pl.pallas_call(
        functools.partial(project_kernel, heads, len(parts)),
        out_shape=jax.ShapeDtypeStruct((rows // heads, columns), BF16),
        in_specs=[vmem] * (len(parts) + 2) + [pl.BlockSpec(memory_space=pl.ANY)],
        out_specs=vmem,
        scratch_shapes=[
            pltpu.VMEM((4, depth, columns // 4), BF16),
            pltpu.VMEM(mixed.shape, F32),
            pltpu.SemaphoreType.DMA((4,)),
        ],
        compiler_params=pltpu.CompilerParams(vmem_limit_bytes=PROJECT_VMEM),
        cost_estimate=pl.CostEstimate(
            flops=5 * 10**8, bytes_accessed=10**7, transcendentals=10**5
        ),
        name="project",
    )(*parts, mixed, log, w_out)


def per_device(
    queries,
    response_keys,
    response_values,
    prompt_keys,
    prompt_value_rows,
    w_out,
    prompt_len,
    resp_len,
):
    tokens, heads, width = queries.shape[1:]
    rows = tokens * heads
    devices = lax.axis_size("grp")
    me = lax.axis_index("grp")
    ring = devices // NEAR

    def send(x, step, flip):
        route = [
            (i, (i // NEAR + step) % ring * NEAR + (i % NEAR ^ flip)) for i in range(devices)
        ]
        return lax.ppermute(x, "grp", route)

    k_mine = prompt_keys.reshape(-1, width)
    v_mine = prompt_value_rows.reshape(-1, width)
    keys = k_mine.shape[0]
    k_other, v_other = send(k_mine, 0, 1), send(v_mine, 0, 1)
    sent = sent_rows(resp_len, jnp.transpose(queries[0], (1, 0, 2)))
    begins = jnp.stack([me, me ^ 1]).astype(jnp.int32) * keys
    valid = jnp.clip(prompt_len[0] - begins, 0, keys)
    prepared = key_part(valid, k_mine, k_other, v_mine, v_other)
    mixed, log = own_part(
        heads,
        sent,
        response_keys.reshape(tokens, width),
        response_values.reshape(tokens, width),
    )
    came = [[send(sent, step, flip) for step, flip in batch] for batch in BATCHES]
    parts = []
    for batch, queries_there in zip(BATCHES, came):
        results = prompt_part(valid, queries_there, *prepared)
        parts += [send(r, -step, flip) for r, (step, flip) in zip(results, batch)]
    parts += prompt_part(valid, [sent], *prepared)
    splits = lax.axis_size("head")
    rows_out = tokens // splits
    partial = project(parts, mixed, log, w_out)
    pieces = lax.all_to_all(
        partial.reshape(splits, rows_out, -1), "head", 0, 0, tiled=True
    )
    summed = jnp.sum(pieces.astype(F32), axis=0)
    first_out = lax.axis_index("head") * rows_out
    live_rows = first_out + jnp.arange(rows_out, dtype=jnp.int32) < resp_len[0]
    return jnp.where(live_rows[:, None], summed, 0.0).astype(BF16)[None]


def solution(mesh):
    in_specs = (
        P("grp", None, "head", None),
        P("grp", None, "head", None),
        P("grp", None, "head", None),
        P("grp", "head", None),
        P("grp", "head", None),
        P("head", None),
        P(),
        P("grp"),
    )
    return jax.shard_map(
        per_device,
        mesh=mesh,
        in_specs=in_specs,
        out_specs=P("grp", "head", None),
        check_vma=False,
    )
```

```python
import functools
import math

import jax
import jax.numpy as jnp
from jax import lax
from jax.experimental import pallas as pl
from jax.experimental.pallas import tpu as pltpu
from jax.sharding import PartitionSpec as P

F32, BF16 = jnp.float32, jnp.bfloat16
LANES = 128
BLOCK_ROWS = 512
TAIL = 16
PROMPT_VMEM = 44 * 2**20
SMALL_VMEM = 16 * 2**20
PROJECT_VMEM = 48 * 2**20
NEAR = 4
BATCHES = (((0, 2), (1, 0), (3, 0)), ((1, 2), (3, 2), (2, 0), (2, 2)))
TO_BASE_2 = math.log2(math.e)
UNSEEN = -1e30
NT = (((1,), (1,)), ((), ()))


def scaled_halves(q, scale):
    scaled = q.astype(F32) * scale
    high = scaled.astype(BF16)
    low = (scaled - high.astype(F32)).astype(BF16)
    return jnp.concatenate([high, low], axis=1)


def diagonal_row(tile):
    eye = lax.broadcasted_iota(jnp.int32, tile.shape, 0) == lax.broadcasted_iota(
        jnp.int32, tile.shape, 1
    )
    return jnp.sum(jnp.where(eye, tile, 0.0), axis=0, keepdims=True)


def log_lines(logs, start, count):
    lines = []
    for j in range(count):
        tile = logs[pl.ds(pl.multiple_of(start + j * LANES, 16), LANES), :]
        lines.append(diagonal_row(tile))
    log = jnp.concatenate(lines, axis=0)
    high = log.astype(BF16).astype(F32)
    middle = (log - high).astype(BF16).astype(F32)
    low = log - high - middle
    spare = jnp.zeros((TAIL - 3 * count, LANES), F32)
    return jnp.concatenate([high, middle, low, spare], axis=0).astype(BF16)


def prompt_kernel(responses, valid_ref, *refs):
    q_refs, refs = refs[:responses], refs[responses:]
    norm_ref, k_ref, v_ref = refs[:3]
    out_refs, refs = refs[3 : 3 + responses], refs[3 + responses :]
    packed, mixed, logs, acc, lowest = refs
    keys, width = k_ref.shape
    keys = keys // 2
    rows = q_refs[0].shape[0] - TAIL
    heads = rows // LANES
    scale = TO_BASE_2 / math.sqrt(width)
    ones = jnp.ones((16, width), BF16)
    key_norm = norm_ref[0:1, 0:1]

    lengths = [
        jnp.max(q_ref[rows:, :].astype(F32)).astype(jnp.int32) for q_ref in q_refs
    ]
    offset = jnp.int32(0)
    offsets = []
    for i, q_ref in enumerate(q_refs):
        offsets.append(offset)
        packed[pl.ds(pl.multiple_of(offset, 16), rows), :] = q_ref[:rows, :]
        offset = offset + (lengths[i] * heads + 15) // 16 * 16
    total = offset
    packed[pl.ds(pl.multiple_of(offsets[-1], 16) + rows, BLOCK_ROWS), :] = jnp.zeros(
        (BLOCK_ROWS, width), BF16
    )
    valid = (valid_ref[0], valid_ref[1])
    some_valid = jnp.maximum(*valid) > 0
    lowest[...] = jnp.ones_like(lowest)

    def block(first, count):
        here = pl.ds(first, count)

        @pl.when(some_valid)
        def _():
            q = packed[here, :]
            squares = lax.dot_general(ones, q * q, NT, preferred_element_type=F32)
            bound = jnp.sqrt(squares[:1, :]) * key_norm
            k = k_ref[...]
            scored = lax.dot_general(
                jnp.concatenate([k, k], axis=1),
                scaled_halves(q, scale),
                NT,
                preferred_element_type=F32,
            )
            weights = jnp.exp2(scored - bound).astype(BF16)
            summed = jnp.dot(v_ref[...], weights, preferred_element_type=F32)
            weight_sum = summed[LANES : LANES + 1, :]
            lowest[:, :count] = jnp.minimum(lowest[:, :count], weight_sum)
            log = jnp.log2(weight_sum) + bound
            mixed[here, :] = (summed[:LANES] * (1.0 / weight_sum)).T
            logs[here, :] = jnp.broadcast_to(log, (LANES, count)).T

        @pl.when(jnp.logical_not(some_valid))
        def _():
            mixed[here, :] = jnp.zeros((count, width), F32)
            logs[here, :] = jnp.full((count, LANES), UNSEEN, F32)

    def exact_block(first, count):
        here = pl.ds(first, count)
        halves = scaled_halves(packed[here, :], scale)
        step = 256

        def over_keys(body, carry):
            def one(c, carry):
                start = pl.multiple_of(c * step, step)
                these = pl.ds(start, step)
                k = k_ref[these, :]
                s = lax.dot_general(
                    halves,
                    jnp.concatenate([k, k], axis=1),
                    NT,
                    preferred_element_type=F32,
                )
                second = start >= keys
                position = lax.broadcasted_iota(jnp.int32, s.shape, 1)
                position = position + (start - jnp.where(second, keys, 0))
                s = jnp.where(position < jnp.where(second, valid[1], valid[0]), s, UNSEEN)
                return body(s, v_ref[:, these], carry)

            return lax.fori_loop(0, 2 * keys // step, one, carry)

        def fold(s, v, peak):
            return jnp.maximum(peak, jnp.max(s, axis=1, keepdims=True))

        peak = over_keys(fold, jnp.full((count, 1), UNSEEN, F32))
        acc[...] = jnp.zeros_like(acc)

        def add(s, v, carry):
            weights = jnp.exp2(s - peak).astype(BF16)
            summed = lax.dot_general(weights, v, NT, preferred_element_type=F32)
            acc[:, :LANES] += summed[:, :LANES]
            acc[:, LANES:] += jnp.broadcast_to(
                summed[:, LANES : LANES + 1], (count, LANES)
            )
            return carry

        over_keys(add, 0)
        weight_sum = acc[:, LANES:]
        mixed[here, :] = acc[:, :LANES] / weight_sum
        logs[here, :] = jnp.log2(weight_sum) + jnp.broadcast_to(peak, (count, LANES))

    half = BLOCK_ROWS // 2
    first = jnp.int32(0)
    if responses > 3:
        double = total // (2 * BLOCK_ROWS)

        @pl.loop(0, double)
        def _(b):
            block(pl.multiple_of(b * (2 * BLOCK_ROWS), BLOCK_ROWS), 2 * BLOCK_ROWS)

        first = double * (2 * BLOCK_ROWS)
    rest = total - first
    spare_rows = rest % BLOCK_ROWS
    big = rest // BLOCK_ROWS + (spare_rows > half).astype(jnp.int32)

    @pl.loop(0, big)
    def _(b):
        block(pl.multiple_of(first + b * BLOCK_ROWS, BLOCK_ROWS), BLOCK_ROWS)

    @pl.when(rest > big * BLOCK_ROWS)
    def _():
        block(pl.multiple_of(first + big * BLOCK_ROWS, BLOCK_ROWS), half)

    @pl.when(jnp.logical_and(some_valid, jnp.logical_not(jnp.min(lowest[...]) > 2.0**-90)))
    def _():
        @pl.loop(0, (total + half - 1) // half)
        def _(b):
            exact_block(pl.multiple_of(b * half, half), half)

    for i, out_ref in enumerate(out_refs):
        start = pl.multiple_of(offsets[i], 16)
        out_ref[:rows, :] = mixed[pl.ds(start, rows), :].astype(BF16)
        out_ref[rows:, :] = log_lines(logs, start, pl.cdiv(rows, LANES))


def prompt_part(valid, queries, norm, k, v):
    responses = len(queries)
    rows, width = queries[0].shape
    vmem = pl.BlockSpec(memory_space=pltpu.VMEM)
    smem = pl.BlockSpec(memory_space=pltpu.SMEM)
    packed_rows = responses * (rows - TAIL) + BLOCK_ROWS + LANES
    return pl.pallas_call(
        functools.partial(prompt_kernel, responses),
        out_shape=(jax.ShapeDtypeStruct((rows, width), BF16),) * responses,
        in_specs=[smem] + [vmem] * (responses + 3),
        out_specs=(vmem,) * responses,
        scratch_shapes=[
            pltpu.VMEM((packed_rows, width), BF16),
            pltpu.VMEM((packed_rows, width), F32),
            pltpu.VMEM((packed_rows, LANES), F32),
            pltpu.VMEM((BLOCK_ROWS // 2, width + LANES), F32),
            pltpu.VMEM((1, 2 * BLOCK_ROWS), F32),
        ],
        compiler_params=pltpu.CompilerParams(vmem_limit_bytes=PROMPT_VMEM),
        cost_estimate=pl.CostEstimate(
            flops=10**8, bytes_accessed=10**6, transcendentals=10**5
        ),
        name="prompt_part",
    )(valid, *queries, norm, k, v)


def key_kernel(valid_ref, k0_ref, k1_ref, v0_ref, v1_ref, norm_ref, k_ref, v_ref):
    keys, width = k0_ref.shape
    ones = jnp.ones((width, LANES), BF16)
    norm = jnp.zeros((1, LANES), F32)
    for part, (key_ref, value_ref) in enumerate(((k0_ref, v0_ref), (k1_ref, v1_ref))):
        here = pl.ds(part * keys, keys)
        key = key_ref[...]
        k_ref[here, :] = key
        squares = jnp.dot(key * key, ones, preferred_element_type=F32)
        norm = jnp.maximum(norm, jnp.max(squares, axis=0, keepdims=True))
        v_ref[:width, here] = value_ref[...].T
        v_ref[width:, here] = jnp.ones((TAIL, keys), BF16)

        @pl.when(valid_ref[part] < keys)
        def _():
            value = v_ref[:, here].astype(F32)
            position = lax.broadcasted_iota(jnp.int32, value.shape, 1)
            v_ref[:, here] = jnp.where(position < valid_ref[part], value, 0.0).astype(BF16)

    scale = TO_BASE_2 / math.sqrt(width)
    norm_ref[...] = jnp.broadcast_to(jnp.sqrt(norm) * (scale * 1.01), norm_ref.shape)


def key_part(valid, k0, k1, v0, v1):
    keys, width = k0.shape
    vmem = pl.BlockSpec(memory_space=pltpu.VMEM)
    smem = pl.BlockSpec(memory_space=pltpu.SMEM)
    return pl.pallas_call(
        key_kernel,
        out_shape=(
            jax.ShapeDtypeStruct((8, LANES), F32),
            jax.ShapeDtypeStruct((2 * keys, width), BF16),
            jax.ShapeDtypeStruct((width + TAIL, 2 * keys), BF16),
        ),
        in_specs=[smem] + [vmem] * 4,
        out_specs=(vmem,) * 3,
        compiler_params=pltpu.CompilerParams(vmem_limit_bytes=SMALL_VMEM),
        cost_estimate=pl.CostEstimate(
            flops=3 * 10**8, bytes_accessed=4 * 10**6, transcendentals=10**3
        ),
        name="key_part",
    )(valid, k0, k1, v0, v1)


def sent_kernel(length_ref, q_ref, out_ref, rows_ref):
    heads, tokens, width = q_ref.shape
    for h in range(heads):
        rows_ref[pl.ds(h, tokens, stride=heads), :] = q_ref[h].astype(F32)
    out_ref[: heads * tokens, :] = rows_ref[...].astype(BF16)
    length = length_ref[0].astype(F32)
    out_ref[heads * tokens :, :] = jnp.full((TAIL, width), length, F32).astype(BF16)


def sent_rows(length, q):
    heads, tokens, width = q.shape
    return pl.pallas_call(
        sent_kernel,
        out_shape=jax.ShapeDtypeStruct((heads * tokens + TAIL, width), BF16),
        in_specs=[
            pl.BlockSpec(memory_space=pltpu.SMEM),
            pl.BlockSpec(memory_space=pltpu.VMEM),
        ],
        out_specs=pl.BlockSpec(memory_space=pltpu.VMEM),
        scratch_shapes=[pltpu.VMEM((heads * tokens, width), F32)],
        compiler_params=pltpu.CompilerParams(vmem_limit_bytes=SMALL_VMEM),
        name="sent_rows",
    )(length, q)


def own_kernel(heads, q_ref, k_ref, v_ref, mixed_ref, log_ref, column):
    rows, width = mixed_ref.shape
    k = k_ref[...]
    kk = jnp.concatenate([k, k], axis=1)
    s = lax.dot_general(
        scaled_halves(q_ref[:rows, :], TO_BASE_2 / math.sqrt(width)),
        kk,
        NT,
        preferred_element_type=F32,
    )
    row = lax.broadcasted_iota(jnp.int32, s.shape, 0)
    position = lax.broadcasted_iota(jnp.int32, s.shape, 1)
    s = jnp.where(position * heads <= row, s, UNSEEN)
    peak = jnp.max(s, axis=1, keepdims=True)
    weights = jnp.exp2(s - peak)
    weight_sum = jnp.sum(weights, axis=1, keepdims=True)
    mixed_ref[...] = (
        jnp.dot(weights.astype(BF16), v_ref[...], preferred_element_type=F32) / weight_sum
    )
    column[...] = jnp.broadcast_to(jnp.log2(weight_sum) + peak, (rows, LANES))
    for j in range(rows // LANES):
        log_ref[j : j + 1, :] = diagonal_row(column[j * LANES : (j + 1) * LANES, :])


def own_part(heads, q, k, v):
    rows, width = q.shape[0] - TAIL, q.shape[1]
    vmem = pl.BlockSpec(memory_space=pltpu.VMEM)
    return pl.pallas_call(
        functools.partial(own_kernel, heads),
        out_shape=(
            jax.ShapeDtypeStruct((rows, width), F32),
            jax.ShapeDtypeStruct((8, LANES), F32),
        ),
        in_specs=[vmem] * 3,
        out_specs=(vmem,) * 2,
        scratch_shapes=[pltpu.VMEM((rows, LANES), F32)],
        compiler_params=pltpu.CompilerParams(vmem_limit_bytes=SMALL_VMEM),
        cost_estimate=pl.CostEstimate(
            flops=10**8, bytes_accessed=10**6, transcendentals=10**5
        ),
        name="own_part",
    )(q, k, v)


def project_kernel(
    heads, count, *refs
):
    part_refs = refs[:count]
    mixed_ref, log_ref, w_hbm, out_ref, w_ref, attended, sems = refs[count:]
    chunks, _, columns = w_ref.shape
    loads = [
        pltpu.make_async_copy(
            w_hbm.at[:, pl.ds(c * columns, columns)], w_ref.at[c], sems.at[c]
        )
        for c in range(chunks)
    ]
    for load in loads:
        load.start()
    rows = part_refs[0].shape[0] - TAIL
    lines_each = pl.cdiv(rows, LANES)
    logs = [log_ref[:lines_each, :]]
    for part_ref in part_refs:
        tail = part_ref[rows:, :].astype(F32)
        logs.append(
            tail[:lines_each]
            + tail[lines_each : 2 * lines_each]
            + tail[2 * lines_each : 3 * lines_each]
        )
    peak = logs[0]
    for log in logs[1:]:
        peak = jnp.maximum(peak, log)
    shares = [jnp.exp2(log - peak) for log in logs]
    total = shares[0]
    for share in shares[1:]:
        total = total + share
    shares = [share / total for share in shares]
    spread_shape = (2 * LANES, len(shares) * LANES)
    spread = jnp.where(
        lax.broadcasted_iota(jnp.int32, spread_shape, 0) % LANES
        == lax.broadcasted_iota(jnp.int32, spread_shape, 1) // LANES,
        1.0,
        0.0,
    ).astype(BF16)
    for j in range(lines_each):
        lines = [share[j : j + 1, :] for share in shares]
        lines.append(jnp.zeros((LANES - len(lines), LANES), F32))
        by_row = jnp.concatenate(lines, axis=0).T
        size = min(LANES, rows - j * LANES)
        here = slice(j * LANES, j * LANES + size)
        by_row = jnp.dot(scaled_halves(by_row, 1.0), spread, preferred_element_type=F32)
        value = mixed_ref[here, :] * by_row[:size, :LANES]
        for p, part_ref in enumerate(part_refs):
            share = by_row[:size, (p + 1) * LANES : (p + 2) * LANES]
            value = value + part_ref[here, :].astype(F32) * share
        attended[here, :] = value
    tokens = rows // heads
    wide = jnp.concatenate(
        [attended[pl.ds(h, tokens, stride=heads), :].astype(BF16) for h in range(heads)],
        axis=1,
    )
    for c in range(chunks):
        loads[c].wait()
        out_ref[:, c * columns : (c + 1) * columns] = jnp.dot(
            wide, w_ref[c], preferred_element_type=F32
        ).astype(BF16)


def project(parts, mixed, log, w_out):
    rows, width = mixed.shape
    depth, columns = w_out.shape
    heads = depth // width
    vmem = pl.BlockSpec(memory_space=pltpu.VMEM)
    return pl.pallas_call(
        functools.partial(project_kernel, heads, len(parts)),
        out_shape=jax.ShapeDtypeStruct((rows // heads, columns), BF16),
        in_specs=[vmem] * (len(parts) + 2) + [pl.BlockSpec(memory_space=pl.ANY)],
        out_specs=vmem,
        scratch_shapes=[
            pltpu.VMEM((4, depth, columns // 4), BF16),
            pltpu.VMEM(mixed.shape, F32),
            pltpu.SemaphoreType.DMA((4,)),
        ],
        compiler_params=pltpu.CompilerParams(vmem_limit_bytes=PROJECT_VMEM),
        cost_estimate=pl.CostEstimate(
            flops=5 * 10**8, bytes_accessed=10**7, transcendentals=10**5
        ),
        name="project",
    )(*parts, mixed, log, w_out)


def per_device(
    queries,
    response_keys,
    response_values,
    prompt_keys,
    prompt_value_rows,
    w_out,
    prompt_len,
    resp_len,
):
    tokens, heads, width = queries.shape[1:]
    rows = tokens * heads
    devices = lax.axis_size("grp")
    me = lax.axis_index("grp")
    ring = devices // NEAR

    def send(x, step, flip):
        route = [
            (i, (i // NEAR + step) % ring * NEAR + (i % NEAR ^ flip)) for i in range(devices)
        ]
        return lax.ppermute(x, "grp", route)

    k_mine = prompt_keys.reshape(-1, width)
    v_mine = prompt_value_rows.reshape(-1, width)
    keys = k_mine.shape[0]
    k_other, v_other = send(k_mine, 0, 1), send(v_mine, 0, 1)
    sent = sent_rows(resp_len, jnp.transpose(queries[0], (1, 0, 2)))
    begins = jnp.stack([me, me ^ 1]).astype(jnp.int32) * keys
    valid = jnp.clip(prompt_len[0] - begins, 0, keys)
    prepared = key_part(valid, k_mine, k_other, v_mine, v_other)
    mixed, log = own_part(
        heads,
        sent,
        response_keys.reshape(tokens, width),
        response_values.reshape(tokens, width),
    )
    came = [[send(sent, step, flip) for step, flip in batch] for batch in BATCHES]
    parts = []
    for batch, queries_there in zip(BATCHES, came):
        results = prompt_part(valid, queries_there, *prepared)
        parts += [send(r, -step, flip) for r, (step, flip) in zip(results, batch)]
    parts += prompt_part(valid, [sent], *prepared)
    splits = lax.axis_size("head")
    rows_out = tokens // splits
    partial = project(parts, mixed, log, w_out)
    pieces = lax.all_to_all(
        partial.reshape(splits, rows_out, -1), "head", 0, 0, tiled=True
    )
    summed = jnp.sum(pieces.astype(F32), axis=0)
    first_out = lax.axis_index("head") * rows_out
    live_rows = first_out + jnp.arange(rows_out, dtype=jnp.int32) < resp_len[0]
    return jnp.where(live_rows[:, None], summed, 0.0).astype(BF16)[None]


def solution(mesh):
    in_specs = (
        P("grp", None, "head", None),
        P("grp", None, "head", None),
        P("grp", None, "head", None),
        P("grp", "head", None),
        P("grp", "head", None),
        P("head", None),
        P(),
        P("grp"),
    )
    return jax.shard_map(
        per_device,
        mesh=mesh,
        in_specs=in_specs,
        out_specs=P("grp", "head", None),
        check_vma=False,
    )
```
